32 devices in a mesh: groups: 2 (over y), expert: 4 (over z), mp: 4 (over x, core), section: 1.
Axes of the slice: x: 2, y: 2, z: 4, core: 2. Of those that a mesh axis runs over, the one named last changes fastest.
Arguments:
- tokens: bfloat16 [4096, 2048], P(('groups', 'expert', 'mp'), 'section'), parts along dimension 0, may hold values from -6 to 6
- expert_ids: int32 [4096, 8], P(('groups', 'expert', 'mp')), parts along dimension 0, may hold values from 0 to 15, all different within a row; in each aligned block of 128 rows (0 to 127, 128 to 255, ...) at most 80 rows name the same one
- route_weights: float32 [4096, 8], P(('groups', 'expert', 'mp')), parts along dimension 0, may hold values from 0.1 to 0.5
- gate_weight: bfloat16 [16, 384, 2048], P(('expert', 'mp'), 'section'), may hold values from -0.125 to 0.125
- up_weight: bfloat16 [16, 384, 2048], P(('expert', 'mp'), 'section'), may hold values from -0.125 to 0.125
- down_weight: bfloat16 [16, 384, 2048], P(('expert', 'mp'), None, 'section'), may hold values from -6 to 6
- mask_code: int32 [16, 96, 2048], P(('expert', 'mp'), None, 'section'), may hold values from 0 to 5
Outputs:
- mixed: bfloat16 [4096, 2048], P(('groups', 'expert', 'mp'), 'section'), parts along dimension 0
- pruned_down: bfloat16 [32, 384, 2048], P(('groups', 'expert', 'mp'), None, 'section'), parts along dimension 0
The draws below stay inside these ranges and needn't reach their ends.
There are 2 independent parts, one for each index of `groups`. The reference program is written for one: setup_inputs(seed, part) draws one part's arguments, and reference() takes and returns one part's arrays. A program takes and returns all parts, laid end to end along the dimension named above; an argument that names none is the same for every part. Nothing has to cross between parts.
Inputs may be any that keep to these rules, and one draw needn't show every extreme that they name: `expert_ids`: each row names 8 different experts, and every expert is named by some row. In each aligned block of 128 rows no expert is named by more than 80 rows, a bound that some block reaches.
All inputs are finite; a program needn't handle non-finite values. Where the reference program divides by a largest or mean magnitude, that divisor is 1e-20 or more.
Results may differ from the reference program's by a relative error of at most 0.011.
Values may be sent and summed in bfloat16 or wider, within the bound.
No kernel may reach another device: no remote copies, remote signals or barrier semaphores. Data moves between devices by JAX's collectives and lax.ppermute only.
A program may use at most 64 MiB of HBM per device.

```python
import math
import jax
import jax.numpy as jnp
import numpy as np
from jax import lax

D = 2048
FF = 384
TOPK = 8
NS = 4
TOK_G = 128
EXPERTS = 16
CAP = 80
SLOTS_E = 1280
TOKENS = 2048
N_EXPERT = 4
N_MP = 4


def plant(result, rng, least, high):
    extent = result.shape
    place = [jax.random.randint(jax.random.fold_in(rng, axis), (), 0, extent[axis]) for axis in range(len(extent))]
    result = result.at[tuple(place)].set(least)
    longest = extent.index(max(extent))
    place[longest] = (place[longest] + 1) % extent[longest]
    return result.at[tuple(place)].set(high)


def shard_levels(own_key, shape, pieces, smallest, largest):
    gain, own = 1.0, jax.random.fold_in(own_key, 6)
    for axis_at, parts in pieces:
        draws = jnp.exp(jax.random.uniform(jax.random.fold_in(own, axis_at), (parts,), jnp.float32, smallest / len(pieces), largest / len(pieces)))
        gain = gain * jnp.repeat(draws, shape[axis_at] // parts).reshape([-1 if axis == axis_at else 1 for axis in range(len(shape))])
    return gain


def routed_block(rng, own, number, rows, number_of, top, most, lean):
    order = jax.random.permutation(rng, number_of)
    crowded, usual = load_shares(number_of, rows * top, most, lean, True), load_shares(number_of, rows * top, most, lean, False)
    places = jnp.arange(number_of)

    def named(tallies, rotation):
        used = int((tallies > 0).sum())
        fixed = max(1, used // 4)
        passed = fixed + (places - fixed + rotation * (used - fixed)) % max(1, number_of - fixed)
        return jnp.zeros((number_of,), jnp.int32).at[order[jnp.where(places < fixed, places, passed)]].set(jnp.asarray(tallies, jnp.int32))

    tallies = jnp.where(number % 4 == 0, named(crowded, number // 4), named(usual, number - number // 4 - 1))
    mixed = jax.random.permutation(jax.random.fold_in(own, 3), number_of)
    giver, taker = mixed[0:number_of // 2 * 2:2], mixed[1:number_of // 2 * 2:2]
    room = jnp.minimum(tallies[giver] - 1, most - tallies[taker]) // 2
    room = jnp.where((giver == order[0]) | (taker == order[0]) | (tallies[taker] == 0), 0, jnp.maximum(room, 0))
    passed = jax.random.randint(jax.random.fold_in(own, 4), (number_of // 2,), 0, 1 << 20) % (room + 1)
    tallies = tallies.at[giver].add(-passed).at[taker].add(passed)
    members = jnp.searchsorted(jnp.cumsum(tallies), jnp.arange(rows * top), side="right").astype(jnp.int32)
    table = members.reshape(top, rows).T
    table = table[jax.random.permutation(jax.random.fold_in(own, 1), rows)]
    rotation = jax.random.randint(jax.random.fold_in(own, 2), (rows, 1), 0, top)
    return jnp.take_along_axis(table, (jnp.arange(top)[None, :] + rotation) % top, axis=1)


def load_shares(count, total, limit, slope, full):
    portions = [(1 << 20) // math.isqrt(rank ** slope) + 1 for rank in range(1, count + 1)]
    largest = limit if full else min(limit, max(-(-total // count), total * portions[0] // sum(portions)))
    least = 1 if total - largest >= count - 1 else 0
    given, surplus = [largest] + [least] * (count - 1), total - largest - least * (count - 1)
    while surplus > 0:
        movable = [i for i in range(1, count) if given[i] < largest] or [i for i in range(1, count) if given[i] < limit]
        mass, budget = sum([portions[i] for i in movable]), surplus
        for i in movable:
            extra = min(limit - given[i], max(1, budget * portions[i] // mass), surplus)
            given[i] = given[i] + extra
            surplus = surplus - extra
    return np.array(given)


def centred(key, shape, deviation, most, cuts=(), kind=jnp.bfloat16):
    values = jax.random.normal(key, shape, jnp.float32) * deviation
    if len(cuts) > 0:
        values = shard_levels(key, shape, cuts, -0.22, 0.18) * values
    return jnp.clip(values, min=-most, max=most).astype(kind)


def setup_inputs(seed: int = 0, part: int = 0) -> dict:
    seeds = jax.random.split(jax.random.key(seed), 8)
    part_keys = jax.random.split(jax.random.fold_in(seeds[7], part), 8)
    tokens = centred(part_keys[0], (TOKENS, D), 1.0, 6.0, ((0, 16),))
    expert_ids_keys = jax.random.split(jax.random.fold_in(part_keys[1], 1), TOKENS // TOK_G)
    expert_ids_turns = jax.random.permutation(jax.random.fold_in(part_keys[1], 3), TOKENS // TOK_G)
    expert_ids = jax.vmap(lambda own, number: routed_block(jax.random.fold_in(part_keys[1], 2), own, number, TOK_G, EXPERTS, TOPK, CAP, 2))(expert_ids_keys, expert_ids_turns).reshape((TOKENS, TOPK))
    route_weights = jnp.clip(0.1 + 0.4 * jax.random.uniform(part_keys[2], (TOKENS, TOPK), jnp.float32) ** shard_levels(part_keys[2], (TOKENS, TOPK), ((0, 16),), -0.2, 0.2), 0.1, 0.5)
    gate_weight = centred(seeds[3], (EXPERTS, FF, D), D ** -0.5, 0.125, ((0, 16),))
    up_weight = centred(seeds[4], (EXPERTS, FF, D), D ** -0.5, 0.125, ((0, 16),))
    down_weight = centred(seeds[5], (EXPERTS, FF, D), 1.0, 6.0, ((0, 16),))
    mask_code = plant(jax.random.randint(seeds[6], (EXPERTS, FF // 4, D), 0, 6), jax.random.fold_in(seeds[6], 1), 0, 5).astype(jnp.int32)
    return dict(tokens=tokens, expert_ids=expert_ids, route_weights=route_weights, gate_weight=gate_weight, up_weight=up_weight, down_weight=down_weight, mask_code=mask_code)


DAMPING = 0.01
EPSILON = 1e-6
PAIR_TABLE = np.array([[1, 1, 0, 0], [1, 0, 1, 0], [1, 0, 0, 1], [0, 1, 1, 0], [0, 1, 0, 1], [0, 0, 1, 1]], dtype=np.float32)


def precise_dot(left, right):
    return jnp.dot(left, right, precision=lax.Precision.HIGHEST, preferred_element_type=jnp.float32)


def decode(code_rows):
    option_count = PAIR_TABLE.shape[0]
    code_hits = (code_rows[:, :, None] == jnp.arange(option_count, dtype=jnp.int32)[None, None, :]).astype(jnp.float32)
    kept_mask = jnp.einsum("gdp,pi->gid", code_hits, jnp.asarray(PAIR_TABLE, jnp.float32))
    return kept_mask.reshape(code_rows.shape[0] * 4, code_rows.shape[1])


def reference(tokens, expert_ids, route_weights, gate_weight, up_weight, down_weight, mask_code):
    group_count = N_EXPERT * N_MP
    flat_ids = expert_ids.reshape(-1)
    blocks = expert_ids.reshape(group_count, TOK_G * TOPK)
    onehot = (blocks[:, :, None] == jnp.arange(EXPERTS, dtype=jnp.int32)[None, None, :]).astype(jnp.int32)
    slot_rank = jnp.sum((jnp.cumsum(onehot, axis=1) - onehot) * onehot, axis=2)
    source = jnp.arange(group_count, dtype=jnp.int32)[:, None]
    slot_index = (source * CAP + slot_rank).reshape(-1).astype(jnp.int32)
    token_index = jnp.arange(TOKENS * TOPK, dtype=jnp.int32) // TOPK
    token_table = jnp.full((EXPERTS, SLOTS_E), TOKENS, jnp.int32).at[flat_ids, slot_index].set(token_index)
    weight_table = jnp.zeros((EXPERTS, SLOTS_E), jnp.float32).at[flat_ids, slot_index].set(route_weights.reshape(-1))
    padded = jnp.concatenate([tokens, jnp.zeros((1, D), tokens.dtype)], axis=0)
    identity = jnp.eye(FF, dtype=jnp.float32)

    def per_expert(combined, inputs):
        row_ids, slot_weights, gate_rows, up_rows, down_rows, code_rows = inputs
        slot_inputs = padded[row_ids]
        gate_pre = jnp.dot(slot_inputs, gate_rows.T, preferred_element_type=jnp.float32)
        up_pre = jnp.dot(slot_inputs, up_rows.T, preferred_element_type=jnp.float32)
        hidden = (jax.nn.silu(gate_pre) * up_pre).astype(jnp.bfloat16)
        gram_matrix = jnp.dot(hidden.T, hidden, preferred_element_type=jnp.float32)
        hessian = gram_matrix + (DAMPING * jnp.mean(jnp.diagonal(gram_matrix)) + EPSILON) * identity
        step_size = 1.0 / jnp.max(jnp.sum(jnp.abs(hessian), axis=1))
        iterate = 2.0 * step_size * identity - step_size * step_size * hessian
        for iteration in range(NS - 1):
            iterate = 2.0 * iterate - precise_dot(precise_dot(iterate, hessian), iterate)
        kept_mask = decode(code_rows)
        weight_wide = down_rows.astype(jnp.float32)
        scaled_error = weight_wide * (1.0 - kept_mask) / jnp.diagonal(iterate)[:, None]
        pruned = (kept_mask * (weight_wide - precise_dot(iterate, scaled_error))).astype(jnp.bfloat16)
        expert_out = (jnp.dot(hidden, pruned, preferred_element_type=jnp.float32) * FF ** -0.5).astype(jnp.bfloat16)
        combined = combined.at[row_ids].add(slot_weights[:, None] * expert_out.astype(jnp.float32), mode="drop")
        return combined, pruned

    combined, pruned_down = lax.scan(per_expert, jnp.zeros((TOKENS, D), jnp.float32), (token_table, weight_table, gate_weight, up_weight, down_weight, mask_code))
    return combined.astype(jnp.bfloat16), pruned_down
```

```python
import functools
import jax
import jax.numpy as jnp
import numpy as np
from jax import lax
from jax.experimental import pallas as pl
from jax.experimental.pallas import tpu as pltpu
from jax.sharding import PartitionSpec as P

FF = 384
NS = 4


DAMPING = 0.01
EPSILON = 1e-06


def decode(mask_code):
    first_row = (mask_code <= 2).astype(jnp.float32)
    second_row = ((mask_code == 0) | (mask_code == 3) | (mask_code == 4)).astype(jnp.float32)
    third_row = ((mask_code == 1) | (mask_code == 3) | (mask_code == 5)).astype(jnp.float32)
    fourth_row = ((mask_code == 2) | (mask_code == 4) | (mask_code == 5)).astype(jnp.float32)
    kept_mask = jnp.stack([first_row, second_row, third_row, fourth_row], axis=2)
    return kept_mask.reshape(mask_code.shape[0], mask_code.shape[1] * 4, mask_code.shape[2])


def precise_matmul(left, right):
    return jnp.einsum(
        "jab,jbc->jac",
        left,
        right,
        precision=lax.Precision.HIGHEST,
        preferred_element_type=jnp.float32,
    )


def routed(tokens, expert_ids, route_weights, gate_weight, up_weight, down_weight, mask_code):
    group_count = lax.axis_size(("expert", "mp"))
    experts_here, half_rows, model_width = gate_weight.shape
    tok_rows, top_count = expert_ids.shape
    experts_all = experts_here * group_count
    capacity = min(tok_rows, 5 * tok_rows * top_count // (4 * experts_all))
    slot_total = group_count * capacity
    flat_ids = expert_ids.reshape(-1)
    onehot = (flat_ids[:, None] == jnp.arange(experts_all, dtype=jnp.int32)[None, :]).astype(
        jnp.int32
    )
    slot_rank = jnp.sum((jnp.cumsum(onehot, axis=0) - onehot) * onehot, axis=1)
    local_expert = flat_ids % experts_here
    position = flat_ids // experts_here * capacity + slot_rank
    token_of = jnp.arange(tok_rows * top_count, dtype=jnp.int32) // top_count
    slot_token = (
        jnp.full((experts_here, slot_total), tok_rows, jnp.int32)
        .at[local_expert, position]
        .set(token_of)
    )
    full_rows = lax.all_gather(tokens, "section", axis=1, tiled=True)
    padded_rows = jnp.concatenate(
        [full_rows, jnp.zeros((1, full_rows.shape[1]), full_rows.dtype)], axis=0
    )
    send_rows = padded_rows[slot_token]
    slot_rows = lax.all_to_all(send_rows, ("expert", "mp"), split_axis=1, concat_axis=1, tiled=True)
    gate_pre = jnp.einsum(
        "jfd,jsd->jfs", gate_weight, slot_rows, preferred_element_type=jnp.float32
    )
    up_pre = jnp.einsum("jfd,jsd->jfs", up_weight, slot_rows, preferred_element_type=jnp.float32)
    hidden_half = (jax.nn.silu(gate_pre) * up_pre).astype(jnp.bfloat16)
    hidden_all = lax.all_gather(hidden_half, "section", axis=1, tiled=True)
    hidden_width = hidden_all.shape[1]
    gram_matrix = jnp.einsum(
        "jfs,jgs->jfg", hidden_all, hidden_all, preferred_element_type=jnp.float32
    )
    mean_diag = jnp.mean(jnp.diagonal(gram_matrix, axis1=1, axis2=2), axis=1)
    identity = jnp.eye(hidden_width, dtype=jnp.float32)
    hessian = gram_matrix + (DAMPING * mean_diag + EPSILON)[:, None, None] * identity
    step_size = 1.0 / jnp.max(jnp.sum(jnp.abs(hessian), axis=2), axis=1)
    iterate = (
        2.0 * step_size[:, None, None] * identity - (step_size * step_size)[:, None, None] * hessian
    )
    for iteration in range(NS - 1):
        iterate = 2.0 * iterate - precise_matmul(precise_matmul(iterate, hessian), iterate)
    kept_mask = decode(mask_code)
    weight_wide = down_weight.astype(jnp.float32)
    inverse_diag = jnp.diagonal(iterate, axis1=1, axis2=2)
    scaled_error = weight_wide * (1.0 - kept_mask) / inverse_diag[:, :, None]
    correction = precise_matmul(iterate, scaled_error)
    pruned = (kept_mask * (weight_wide - correction)).astype(jnp.bfloat16)
    expert_out = (
        jnp.einsum("jfs,jfd->jsd", hidden_all, pruned, preferred_element_type=jnp.float32)
        * FF ** (-0.5)
    ).astype(jnp.bfloat16)
    returned = lax.all_to_all(expert_out, ("expert", "mp"), split_axis=1, concat_axis=1, tiled=True)
    picked = returned[local_expert, position].reshape(tok_rows, top_count, -1)
    combined = jnp.einsum("tkd,tk->td", picked.astype(jnp.float32), route_weights)
    return (combined.astype(jnp.bfloat16), pruned)


AXES = ("expert", "mp")
CHUNK = 128
BF = jnp.bfloat16
F32 = jnp.float32


def params(*semantics):
    return pltpu.CompilerParams(
        dimension_semantics=semantics or None, vmem_limit_bytes=40 * 1024 * 1024
    )


def whole(shape):
    return pl.BlockSpec(shape, lambda *_: (0,) * len(shape))


def dot(left, right, on=((1,), (0,))):
    return lax.dot_general(left, right, (on, ((), ())), preferred_element_type=F32)


def weight_table(expert_ids, route_weights, experts_all):
    hit = expert_ids[None] == jnp.arange(experts_all, dtype=jnp.int32)[:, None, None]
    return jnp.max(jnp.where(hit, route_weights[None], -1.0), axis=2)


def pick_kernel(blocks, place_ref, table_ref, out_ref):
    rows = []
    for k in range(blocks):
        for which in range(2):
            rows.append(table_ref[pl.ds(place_ref[2 * k + which], 1), :])
    out_ref[...] = jnp.concatenate(rows, axis=0).T


def pick(place, table, blocks):
    tok_rows = table.shape[1]
    return pl.pallas_call(
        functools.partial(pick_kernel, blocks),
        out_shape=jax.ShapeDtypeStruct((tok_rows, 2 * blocks), F32),
        grid_spec=pltpu.PrefetchScalarGridSpec(
            num_scalar_prefetch=1,
            grid=(1,),
            in_specs=[whole(table.shape)],
            out_specs=whole((tok_rows, 2 * blocks)),
        ),
        compiler_params=params("arbitrary"),
        name="pick",
    )(place, table)


def mask_kernel(code_ref, down_ref, kept_ref, error_ref):
    rows, groups = down_ref.shape[0], code_ref.shape[0]
    row = lax.broadcasted_iota(jnp.int32, (rows, groups), 0)
    column = lax.broadcasted_iota(jnp.int32, (rows, groups), 1)
    spread = (row // 4 == column).astype(BF)
    code = dot(spread, code_ref[...].astype(F32).astype(BF))
    place = lax.broadcasted_iota(jnp.int32, code.shape, 0) % 4
    first = code <= 2.5
    second = (code < 0.5) | ((code > 2.5) & (code < 4.5))
    third = ((code > 0.5) & (code < 1.5)) | ((code > 2.5) & (code < 3.5)) | (code > 4.5)
    fourth = ((code > 1.5) & (code < 2.5)) | (code > 3.5)
    kept = jnp.where(
        place == 0,
        first.astype(F32),
        jnp.where(
            place == 1,
            second.astype(F32),
            jnp.where(place == 2, third.astype(F32), fourth.astype(F32)),
        ),
    )
    kept_ref[...] = kept.astype(BF)
    error_ref[...] = (down_ref[...].astype(F32) * (1.0 - kept)).astype(BF)


def masks(code, down):
    groups, width = code.shape
    rows = down.shape[0]
    cut = 512
    spec = pl.BlockSpec((rows, cut), lambda i: (0, i))
    return pl.pallas_call(
        mask_kernel,
        out_shape=[jax.ShapeDtypeStruct((rows, width), BF)] * 2,
        grid=(width // cut,),
        in_specs=[pl.BlockSpec((groups, cut), lambda i: (0, i)), spec],
        out_specs=[spec, spec],
        compiler_params=params("arbitrary"),
        name="masks",
    )(code, down)


def hidden_kernel(pieces, columns, has_gram, *refs):
    x_refs, refs = refs[:pieces], refs[pieces:]
    gate_ref, up_ref, weight_ref, refs = refs[0], refs[1], refs[2], refs[3:]
    gram_in, refs = (refs[0], refs[1:]) if has_gram else (None, refs)
    out_ref, gram_ref, hidden_ref = refs
    step = pl.program_id(0)
    rows = jnp.concatenate([x[...] for x in x_refs], axis=0)
    both = jnp.concatenate([gate_ref[...], up_ref[...]], axis=0)
    pre = dot(rows, both, ((1,), (1,)))
    gate, up = pre[:, :CHUNK], pre[:, CHUNK:]
    weight = jnp.concatenate([weight_ref[:, c : c + 1] for c in columns], axis=0)
    value = gate / (1.0 + jnp.exp(-gate)) * up
    value = jnp.where(weight >= 0.0, value, 0.0).astype(BF)
    hidden_ref[:, pl.ds(pl.multiple_of(step * CHUNK, CHUNK), CHUNK)] = value
    out_ref[...] = (value.astype(F32) * (weight * FF ** (-0.5))).astype(BF)

    @pl.when(step == pl.num_programs(0) - 1)
    def _():
        hidden = hidden_ref[...]
        gram = dot(hidden, hidden, ((0,), (0,)))
        gram_ref[...] = gram if gram_in is None else gram_in[...] + gram


def hidden_part(pieces, gate, up, weights, columns, gram):
    rows = sum(p.shape[0] for p in pieces)
    ff, width = gate.shape
    steps = ff // CHUNK
    slab = pl.BlockSpec((CHUNK, width), lambda i: (i, 0))
    given = list(pieces) + [gate, up, weights] + ([] if gram is None else [gram])
    specs = [whole(p.shape) for p in pieces] + [slab, slab, whole(weights.shape)]
    specs += [] if gram is None else [whole(gram.shape)]
    return pl.pallas_call(
        functools.partial(hidden_kernel, len(pieces), columns, gram is not None),
        out_shape=[
            jax.ShapeDtypeStruct((rows, ff), BF),
            jax.ShapeDtypeStruct((ff, ff), F32),
        ],
        grid=(steps,),
        in_specs=specs,
        out_specs=[pl.BlockSpec((rows, CHUNK), lambda i: (0, i)), whole((ff, ff))],
        scratch_shapes=[pltpu.VMEM((rows, ff), BF)],
        compiler_params=params("arbitrary"),
        cost_estimate=pl.CostEstimate(
            flops=4 * rows * ff * width,
            bytes_accessed=2 * (rows + 2 * ff) * width,
            transcendentals=rows * ff,
        ),
        name="hidden",
    )(*given)


def halves(value):
    high = value.astype(BF)
    return high, (value - high.astype(F32)).astype(BF)


def product(left, right):
    (a, b), (c, d) = left, right
    return dot(a, c) + (dot(a, d) + dot(b, c))


def prune_kernel(own_ref, other_ref, error_ref, down_ref, kept_ref, out_ref, high_ref, low_ref):
    gram = own_ref[...] + other_ref[...]
    size = gram.shape[0]
    row = lax.broadcasted_iota(jnp.int32, (size, size), 0)
    column = lax.broadcasted_iota(jnp.int32, (size, size), 1)
    eye = row == column
    mean_diag = jnp.sum(jnp.where(eye, gram, 0.0)) * (1.0 / size)
    hessian = gram + jnp.where(eye, DAMPING * mean_diag + EPSILON, 0.0)
    step_size = 1.0 / jnp.max(jnp.sum(jnp.abs(hessian), axis=0, keepdims=True))
    scaled = step_size * hessian
    iterate = jnp.where(eye, 2.0, 0.0) - scaled
    parts = halves(scaled)
    scaled = 2.0 * scaled - product(parts, parts)
    for iteration in range(NS - 1):
        parts = halves(scaled)
        if iteration < NS - 2:
            stack = jnp.concatenate([iterate, scaled], axis=0)
            stack = 2.0 * stack - product(halves(stack), parts)
            iterate, scaled = stack[:size], stack[size:]
        else:
            iterate = 2.0 * iterate - product(halves(iterate), parts)
    diag = jnp.sum(jnp.where(eye, iterate, 0.0), axis=0, keepdims=True)
    high, low = halves(iterate / diag)
    high_ref[...] = high
    low_ref[...] = low
    correct(high, low, error_ref, down_ref, kept_ref, out_ref)


def correct(high, low, error_ref, down_ref, kept_ref, out_ref):
    error = error_ref[...]
    correction = dot(high, error) + dot(low, error)
    value = kept_ref[...].astype(F32) * (down_ref[...].astype(F32) - correction)
    out_ref[...] = value.astype(BF)


def correct_kernel(high_ref, low_ref, error_ref, down_ref, kept_ref, out_ref):
    correct(high_ref[...], low_ref[...], error_ref, down_ref, kept_ref, out_ref)


def prune_first(own, other, error, down, kept, cut):
    size = own.shape[0]
    half = pl.BlockSpec((size, cut), lambda i: (0, 0))
    square = whole((size, size))
    return pl.pallas_call(
        prune_kernel,
        out_shape=[jax.ShapeDtypeStruct((size, cut), BF)]
        + [jax.ShapeDtypeStruct((size, size), BF)] * 2,
        grid=(1,),
        in_specs=[square, square, half, half, half],
        out_specs=[half, square, square],
        compiler_params=params("arbitrary"),
        name="prune",
    )(own, other, error, down, kept)


def prune_next(high, low, error, down, kept, cut, at):
    size = high.shape[0]
    half = pl.BlockSpec((size, cut), lambda i: (0, at))
    square = whole((size, size))
    return pl.pallas_call(
        correct_kernel,
        out_shape=jax.ShapeDtypeStruct((size, cut), BF),
        grid=(1,),
        in_specs=[square, square, half, half, half],
        out_specs=whole((size, cut)),
        compiler_params=params("arbitrary"),
        name="prune_next",
    )(high, low, error, down, kept)


def outputs_kernel(block, arrived, own_hidden, other_hidden, own_ref, other_ref, *refs):
    total = dot(own_hidden[...], own_ref[...]) + dot(other_hidden[...], other_ref[...])
    first, second = total[:block], total[block:]
    if arrived:
        size = refs[0].shape[0]
        from_right, from_left = refs[0][...].astype(F32), refs[1][...].astype(F32)
        if size < block:
            empty = jnp.zeros((block - size, total.shape[1]), F32)
            from_left = jnp.concatenate([from_left, empty], axis=0)
            from_right = jnp.concatenate([empty, from_right], axis=0)
        first, second = first + from_right, second + from_left
    refs[-2][...] = first.astype(BF)
    refs[-1][...] = second.astype(BF)


def outputs(own_hidden, other_hidden, own, other, arrived):
    rows = own_hidden.shape[0]
    cut = own.shape[1]
    given = (own_hidden, other_hidden, own, other) + arrived
    return pl.pallas_call(
        functools.partial(outputs_kernel, rows // 2, len(arrived)),
        out_shape=[jax.ShapeDtypeStruct((rows // 2, cut), BF)] * 2,
        grid=(1,),
        in_specs=[whole(g.shape) for g in given],
        out_specs=[whole((rows // 2, cut))] * 2,
        compiler_params=params("arbitrary"),
        cost_estimate=pl.CostEstimate(
            flops=4 * rows * own.shape[0] * cut,
            bytes_accessed=sum(g.size * 2 for g in given) + rows * cut * 2,
            transcendentals=0,
        ),
        name="outputs",
    )(*given)


def self_kernel(own_hidden, other_hidden, own_ref, other_ref, out_ref):
    out_ref[...] = dot(own_hidden[...], own_ref[...]) + dot(other_hidden[...], other_ref[...])


def self_outputs(own_hidden, other_hidden, own, other):
    rows, cut = own_hidden.shape[0], own.shape[1]
    given = (own_hidden, other_hidden, own, other)
    return pl.pallas_call(
        self_kernel,
        out_shape=jax.ShapeDtypeStruct((rows, cut), F32),
        grid=(1,),
        in_specs=[whole(g.shape) for g in given],
        out_specs=whole((rows, cut)),
        compiler_params=params("arbitrary"),
        name="self_outputs",
    )(*given)


def finish_kernel(own_ref, right_ref, left_ref, *refs):
    total = own_ref[...] + right_ref[...].astype(F32) + left_ref[...].astype(F32)
    refs[-1][...] = total.astype(BF)


def finish(own, right, left, width, at, result):
    rows, cut = own.shape
    given = (own, right, left) + (() if result is None else (result,))
    return pl.pallas_call(
        finish_kernel,
        out_shape=jax.ShapeDtypeStruct((rows, width), BF),
        grid=(1,),
        in_specs=[whole((rows, cut))] * 3
        + ([] if result is None else [pl.BlockSpec(memory_space=pl.ANY)]),
        out_specs=pl.BlockSpec((rows, cut), lambda i: (0, at)),
        input_output_aliases={} if result is None else {3: 0},
        compiler_params=params("arbitrary"),
        name="finish",
    )(*given)


def ring_of(expert_size, mp_size):
    chips = mp_size // 2
    order = [(z, 0) for z in range(expert_size)]
    for z in reversed(range(expert_size)):
        side = list(range(1, chips)) if (expert_size - 1 - z) % 2 == 0 else list(range(chips - 1, 0, -1))
        order += [(z, x) for x in side]
    return [z * mp_size + 2 * x for z, x in order]


def dense(expert_size, mp_size, tokens, expert_ids, route_weights, gate, up, down, code):
    gate, up, down, code = gate[0], up[0], down[0], code[0]
    tok_rows, width = tokens.shape
    devices = expert_size * mp_size
    ring = ring_of(expert_size, mp_size)
    length = len(ring)
    reach = length // 2
    here = lax.axis_index(AXES)
    core = here % 2
    position = np.zeros((devices,), np.int32)
    for i, base in enumerate(ring):
        position[base] = position[base + 1] = i
    position = jnp.asarray(position)[here]

    def shift(value, by):
        pairs = [
            (ring[i] + c, ring[(i + by) % length] + c) for i in range(length) for c in range(2)
        ]
        return lax.ppermute(value, AXES, pairs)

    def swap(value):
        return lax.ppermute(value, AXES, [(i, i ^ 1) for i in range(devices)])

    table = weight_table(expert_ids, route_weights, devices)
    gate_other, up_other = swap(gate), swap(up)
    table = lax.all_gather(table, AXES, axis=0, tiled=True)
    around = jnp.asarray(np.array(ring + ring, np.int32))
    sources = lax.dynamic_slice(around, (position,), (length,)) + core
    place = (sources[:, None] * devices + jnp.stack([here, here ^ 1])[None, :]).reshape(-1)
    weights = pick(place.astype(jnp.int32), table, length)

    half = tok_rows // 2
    top, bottom = tokens[:half], tokens[half:]
    right, left = [top, bottom], [top, bottom]
    hidden_own, hidden_other = [], []
    gram_own = gram_other = None

    def add(pieces, blocks):
        nonlocal gram_own, gram_other
        value, gram_other = hidden_part(
            pieces, gate_other, up_other, weights, [2 * b + 1 for b in blocks], gram_other
        )
        hidden_other.append(value)
        value, gram_own = hidden_part(pieces, gate, up, weights, [2 * b for b in blocks], gram_own)
        hidden_own.append(value)

    arrivals = []
    for hop in range(1, reach + 1):
        right[0] = shift(right[0], 1)
        left[1] = shift(left[1], -1)
        if hop < reach:
            right[1] = shift(right[1], 1)
            left[0] = shift(left[0], -1)
            arrivals.append(((*right, *left), (length - hop, hop)))
        else:
            arrivals.append(((right[0], left[1]), (hop,)))
    kept, error = masks(code, down)
    add((tokens,), (0,))
    for pieces, blocks in arrivals:
        add(pieces, blocks)

    gram_other = swap(gram_other)
    cut = width // 2
    pruned = [None, None]
    pruned[0], high, low = prune_first(gram_own, gram_other, error, down, kept, cut)
    pruned_other = [swap(pruned[0]), None]
    pruned[1] = prune_next(high, low, error, down, kept, cut, 1)
    pruned_other[1] = swap(pruned[1])

    moving = [(), ()]
    for hop in range(reach, 0, -1):
        for at in range(2):
            sent = outputs(
                hidden_own[hop], hidden_other[hop], pruned[at], pruned_other[at], moving[at]
            )
            go_left, go_right = sent if hop < reach else (sent[1], sent[0])
            moving[at] = (shift(go_left, -1), shift(go_right, 1))
    mixed = None
    for at in range(2):
        own = self_outputs(hidden_own[0], hidden_other[0], pruned[at], pruned_other[at])
        mixed = finish(own, *moving[at], width, at, mixed)
    return mixed, jnp.concatenate(pruned, axis=1)[None]


def local(expert_size, mp_size, section_size, *given):
    tokens, expert_ids, _, gate_weight = given[:4]
    devices = expert_size * mp_size
    if (
        section_size == 1
        and gate_weight.shape[0] == 1
        and 2 * expert_ids.shape[1] >= devices
        and mp_size % 2 == 0
        and devices >= 8
    ):
        return dense(expert_size, mp_size, *given)
    return routed(*given)


def solution(mesh):
    placed = (
        P(("groups", "expert", "mp"), "section"),
        P(("groups", "expert", "mp"), None),
        P(("groups", "expert", "mp"), None),
        P(("expert", "mp"), "section", None),
        P(("expert", "mp"), "section", None),
        P(("expert", "mp"), None, "section"),
        P(("expert", "mp"), None, "section"),
    )
    sizes = mesh.shape
    return jax.shard_map(
        functools.partial(local, sizes["expert"], sizes["mp"], sizes["section"]),
        mesh=mesh,
        in_specs=placed,
        out_specs=(
            P(("groups", "expert", "mp"), "section"),
            P(("groups", "expert", "mp"), None, "section"),
        ),
        check_vma=False,
    )
```

```python
import functools
import jax
import jax.numpy as jnp
import numpy as np
from jax import lax
from jax.experimental import pallas as pl
from jax.experimental.pallas import tpu as pltpu
from jax.sharding import PartitionSpec as P

FF = 384
NS = 4


DAMPING = 0.01
EPSILON = 1e-06


def decode(mask_code):
    first_row = (mask_code <= 2).astype(jnp.float32)
    second_row = ((mask_code == 0) | (mask_code == 3) | (mask_code == 4)).astype(jnp.float32)
    third_row = ((mask_code == 1) | (mask_code == 3) | (mask_code == 5)).astype(jnp.float32)
    fourth_row = ((mask_code == 2) | (mask_code == 4) | (mask_code == 5)).astype(jnp.float32)
    kept_mask = jnp.stack([first_row, second_row, third_row, fourth_row], axis=2)
    return kept_mask.reshape(mask_code.shape[0], mask_code.shape[1] * 4, mask_code.shape[2])


def precise_matmul(left, right):
    return jnp.einsum(
        "jab,jbc->jac",
        left,
        right,
        precision=lax.Precision.HIGHEST,
        preferred_element_type=jnp.float32,
    )


def routed(tokens, expert_ids, route_weights, gate_weight, up_weight, down_weight, mask_code):
    group_count = lax.axis_size(("expert", "mp"))
    experts_here, half_rows, model_width = gate_weight.shape
    tok_rows, top_count = expert_ids.shape
    experts_all = experts_here * group_count
    capacity = min(tok_rows, 5 * tok_rows * top_count // (4 * experts_all))
    slot_total = group_count * capacity
    flat_ids = expert_ids.reshape(-1)
    onehot = (flat_ids[:, None] == jnp.arange(experts_all, dtype=jnp.int32)[None, :]).astype(
        jnp.int32
    )
    slot_rank = jnp.sum((jnp.cumsum(onehot, axis=0) - onehot) * onehot, axis=1)
    local_expert = flat_ids % experts_here
    position = flat_ids // experts_here * capacity + slot_rank
    token_of = jnp.arange(tok_rows * top_count, dtype=jnp.int32) // top_count
    slot_token = (
        jnp.full((experts_here, slot_total), tok_rows, jnp.int32)
        .at[local_expert, position]
        .set(token_of)
    )
    full_rows = lax.all_gather(tokens, "section", axis=1, tiled=True)
    padded_rows = jnp.concatenate(
        [full_rows, jnp.zeros((1, full_rows.shape[1]), full_rows.dtype)], axis=0
    )
    send_rows = padded_rows[slot_token]
    slot_rows = lax.all_to_all(send_rows, ("expert", "mp"), split_axis=1, concat_axis=1, tiled=True)
    gate_pre = jnp.einsum(
        "jfd,jsd->jfs", gate_weight, slot_rows, preferred_element_type=jnp.float32
    )
    up_pre = jnp.einsum("jfd,jsd->jfs", up_weight, slot_rows, preferred_element_type=jnp.float32)
    hidden_half = (jax.nn.silu(gate_pre) * up_pre).astype(jnp.bfloat16)
    hidden_all = lax.all_gather(hidden_half, "section", axis=1, tiled=True)
    hidden_width = hidden_all.shape[1]
    gram_matrix = jnp.einsum(
        "jfs,jgs->jfg", hidden_all, hidden_all, preferred_element_type=jnp.float32
    )
    mean_diag = jnp.mean(jnp.diagonal(gram_matrix, axis1=1, axis2=2), axis=1)
    identity = jnp.eye(hidden_width, dtype=jnp.float32)
    hessian = gram_matrix + (DAMPING * mean_diag + EPSILON)[:, None, None] * identity
    step_size = 1.0 / jnp.max(jnp.sum(jnp.abs(hessian), axis=2), axis=1)
    iterate = (
        2.0 * step_size[:, None, None] * identity - (step_size * step_size)[:, None, None] * hessian
    )
    for iteration in range(NS - 1):
        iterate = 2.0 * iterate - precise_matmul(precise_matmul(iterate, hessian), iterate)
    kept_mask = decode(mask_code)
    weight_wide = down_weight.astype(jnp.float32)
    inverse_diag = jnp.diagonal(iterate, axis1=1, axis2=2)
    scaled_error = weight_wide * (1.0 - kept_mask) / inverse_diag[:, :, None]
    correction = precise_matmul(iterate, scaled_error)
    pruned = (kept_mask * (weight_wide - correction)).astype(jnp.bfloat16)
    expert_out = (
        jnp.einsum("jfs,jfd->jsd", hidden_all, pruned, preferred_element_type=jnp.float32)
        * FF ** (-0.5)
    ).astype(jnp.bfloat16)
    returned = lax.all_to_all(expert_out, ("expert", "mp"), split_axis=1, concat_axis=1, tiled=True)
    picked = returned[local_expert, position].reshape(tok_rows, top_count, -1)
    combined = jnp.einsum("tkd,tk->td", picked.astype(jnp.float32), route_weights)
    return (combined.astype(jnp.bfloat16), pruned)


AXES = ("expert", "mp")
CHUNK = 128
EXTRA = 8
BF = jnp.bfloat16
F32 = jnp.float32


def params(*semantics, mib=16):
    return pltpu.CompilerParams(
        dimension_semantics=semantics or None, vmem_limit_bytes=mib * 1024 * 1024
    )


def whole(shape):
    return pl.BlockSpec(shape, lambda *_: (0,) * len(shape))


def dot(left, right, on=((1,), (0,))):
    return lax.dot_general(left, right, (on, ((), ())), preferred_element_type=F32)


def split_kernel(experts_all, x_ref, ids_ref, weight_ref, *out_refs):
    half = x_ref.shape[0] // 2
    ids, weight = ids_ref[...], weight_ref[...]
    table = [
        jnp.max(jnp.where(ids == e, weight, -1.0), axis=0, keepdims=True)
        for e in range(experts_all)
    ]
    table = jnp.concatenate(table, axis=0)
    high = table.astype(BF).astype(F32)
    both = jnp.concatenate([high, table - high], axis=0)
    parts = [both[i : i + EXTRA] for i in range(0, 2 * experts_all, EXTRA)]
    lanes = both.shape[1]
    rest = x_ref.shape[1] - len(parts) * lanes
    extra = jnp.concatenate(parts + [jnp.zeros((EXTRA, rest), F32)], axis=1).astype(BF)
    for at, (wide, plain) in enumerate(((out_refs[0], out_refs[3]), (out_refs[1], out_refs[2]))):
        value = x_ref[at * half : (at + 1) * half, :]
        wide[:half, :] = value
        wide[half:, :] = extra
        plain[...] = value


def split(tokens, expert_ids, route_weights, experts_all):
    rows, width = tokens.shape
    wide = jax.ShapeDtypeStruct((rows // 2 + EXTRA, width), BF)
    plain = jax.ShapeDtypeStruct((rows // 2, width), BF)
    given = (tokens, expert_ids.T, route_weights.T)
    return pl.pallas_call(
        functools.partial(split_kernel, experts_all),
        out_shape=[wide, wide, plain, plain],
        grid=(1,),
        in_specs=[whole(g.shape) for g in given],
        out_specs=[whole(o.shape) for o in (wide, wide, plain, plain)],
        compiler_params=params("arbitrary", mib=56),
        name="split",
    )(*given)


def token_weights(ref, experts_all, expert):
    half, lanes = ref.shape[0] - EXTRA, 2 * (ref.shape[0] - EXTRA)
    count = 2 * experts_all // EXTRA
    parts = [ref[half:, i * lanes : (i + 1) * lanes].astype(F32) for i in range(count)]
    both = jnp.concatenate(parts, axis=0)
    table = both[:experts_all] + both[experts_all:]
    row = lax.broadcasted_iota(jnp.int32, table.shape, 0)
    return jnp.sum(jnp.where(row == expert, table, 0.0), axis=0, keepdims=True)


def mask_kernel(code_ref, down_ref, kept_ref, error_ref):
    rows, groups = down_ref.shape[0], code_ref.shape[0]
    code = code_ref[...]
    first = code <= 2
    second = (code == 0) | (code == 3) | (code == 4)
    third = (code == 1) | (code == 3) | (code == 5)
    fourth = (code == 2) | (code == 4) | (code == 5)
    planes = [jnp.where(plane, 1.0, 0.0).astype(BF) for plane in (first, second, third, fourth)]
    row = lax.broadcasted_iota(jnp.int32, (rows, rows), 0)
    column = lax.broadcasted_iota(jnp.int32, (rows, rows), 1)
    spread = jnp.where(row % 4 * groups + row // 4 == column, 1.0, 0.0).astype(BF)
    kept = dot(spread, jnp.concatenate(planes, axis=0))
    kept_ref[...] = kept.astype(BF)
    error_ref[...] = jnp.where(kept > 0.5, 0.0, down_ref[...].astype(F32)).astype(BF)


def masks(code, down):
    groups, width = code.shape
    rows = down.shape[0]
    cut = 512
    spec = pl.BlockSpec((rows, cut), lambda i: (0, i))
    return pl.pallas_call(
        mask_kernel,
        out_shape=[jax.ShapeDtypeStruct((rows, width), BF)] * 2,
        grid=(width // cut,),
        in_specs=[pl.BlockSpec((groups, cut), lambda i: (0, i)), spec],
        out_specs=[spec, spec],
        compiler_params=params("arbitrary"),
        cost_estimate=pl.CostEstimate(
            flops=2 * rows * rows * width, bytes_accessed=8 * rows * width, transcendentals=0
        ),
        name="masks",
    )(code, down)


def hidden_kernel(pieces, sources, experts, experts_all, has_gram, place_ref, *refs):
    count = len(experts)
    x_refs, refs = refs[:pieces], refs[pieces:]
    pairs, grams_in = refs[: 2 * count], refs[2 * count : 3 * count]
    out_ref, gram_refs, rows_ref, weight_ref, hidden_ref = (
        refs[-4 - count],
        refs[-3 - count : -3],
        *refs[-3:],
    )
    steps = pl.num_programs(0) // count

    def work(which, step):
        @pl.when(step == 0)
        def _():
            half = min(x.shape[0] for x in x_refs)
            half = half - half % 16
            if which == 0:
                for at, x in enumerate(x_refs):
                    rows_ref[at * half : (at + 1) * half, :] = x[:half, :]
            expert = place_ref[experts[which]]
            weight = [token_weights(x_refs[i], experts_all, expert) for i in sources]
            tok_rows = weight[0].shape[1]
            empty = jnp.zeros((8 - len(sources), tok_rows), F32)
            weight = jnp.concatenate(weight + [empty], axis=0).T
            for at in range(len(sources)):
                weight_ref[at * tok_rows : (at + 1) * tok_rows, :] = jnp.broadcast_to(
                    weight[:, at : at + 1], (tok_rows, CHUNK)
                )

        at = pl.ds(pl.multiple_of(step * CHUNK, CHUNK), CHUNK)
        gate_ref, up_ref = pairs[2 * which], pairs[2 * which + 1]
        both = jnp.concatenate([gate_ref[at, :], up_ref[at, :]], axis=0)
        pre = dot(rows_ref[...], both, ((1,), (1,)))
        gate, up = pre[:, :CHUNK], pre[:, CHUNK:]
        weight = weight_ref[...]
        value = gate / (1.0 + jnp.exp(-gate)) * up
        value = jnp.where(weight >= 0.0, value, 0.0).astype(BF)
        hidden_ref[:, at] = value
        out_ref[...] = (value.astype(F32) * (weight * FF ** (-0.5))).astype(BF)

        @pl.when(step == steps - 1)
        def _():
            hidden = hidden_ref[...]
            gram = dot(hidden, hidden, ((0,), (0,)))
            gram_refs[which][...] = grams_in[which][...] + gram if has_gram else gram

    step = pl.program_id(0)
    if count == 1:
        work(0, step)
    else:
        for which in range(count):
            pl.when(step // steps == which)(functools.partial(work, which, step - which * steps))


def hidden_part(place, experts, experts_all, pieces, sources, pairs, grams):
    half = min(p.shape[0] for p in pieces)
    rows = len(pieces) * (half - half % 16)
    ff, width = pairs[0][0].shape
    count = len(experts)
    resident = pl.BlockSpec(memory_space=pltpu.VMEM)
    given = [*pieces] + [w for pair in pairs for w in pair] + [*grams]
    specs = [resident] * (len(pieces) + 2 * count + len(grams))
    return pl.pallas_call(
        functools.partial(
            hidden_kernel, len(pieces), sources, experts, experts_all, len(grams) > 0
        ),
        out_shape=[jax.ShapeDtypeStruct((rows, count * ff), BF)]
        + [jax.ShapeDtypeStruct((ff, ff), F32)] * count,
        grid_spec=pltpu.PrefetchScalarGridSpec(
            num_scalar_prefetch=1,
            grid=(count * ff // CHUNK,),
            in_specs=specs,
            out_specs=[pl.BlockSpec((rows, CHUNK), lambda i, _: (0, i))]
            + [whole((ff, ff))] * count,
            scratch_shapes=[
                pltpu.VMEM((rows, width), BF),
                pltpu.VMEM((rows, CHUNK), F32),
                pltpu.VMEM((rows, ff), BF),
            ],
        ),
        compiler_params=params("arbitrary"),
        cost_estimate=pl.CostEstimate(
            flops=4 * rows * ff * width * count,
            bytes_accessed=2 * (rows + 2 * ff * count) * width,
            transcendentals=rows * ff * count,
        ),
        name="hidden",
    )(place, *given)


def product(left, right):
    return dot(left.astype(BF), right)


def prune_kernel(own_ref, other_ref, error_ref, down_ref, kept_ref, out_ref, inverse_ref):
    gram = own_ref[...] + other_ref[...]
    size = gram.shape[0]
    row = lax.broadcasted_iota(jnp.int32, (size, size), 0)
    column = lax.broadcasted_iota(jnp.int32, (size, size), 1)
    eye = row == column
    mean_diag = jnp.sum(jnp.where(eye, gram, 0.0)) * (1.0 / size)
    hessian = gram + jnp.where(eye, DAMPING * mean_diag + EPSILON, 0.0)
    step_size = 1.0 / jnp.max(jnp.sum(jnp.abs(hessian), axis=0, keepdims=True))
    scaled = step_size * hessian
    iterate = jnp.where(eye, 2.0, 0.0) - scaled
    right = scaled.astype(BF)
    scaled = 2.0 * scaled - dot(right, right)
    for iteration in range(NS - 1):
        right = scaled.astype(BF)
        following = 2.0 * iterate - product(iterate, right)
        if iteration < NS - 2:
            scaled = 2.0 * scaled - dot(right, right)
        iterate = following
    diag = jnp.sum(jnp.where(eye, iterate, 0.0), axis=0, keepdims=True)
    inverse_ref[...] = (iterate * (1.0 / diag)).astype(BF)
    correct_kernel(inverse_ref, error_ref, down_ref, kept_ref, out_ref)


def correct_kernel(inverse_ref, error_ref, down_ref, kept_ref, out_ref):
    correction = dot(inverse_ref[...], error_ref[...])
    value = kept_ref[...].astype(F32) * (down_ref[...].astype(F32) - correction)
    out_ref[...] = value.astype(BF)


def prune_cost(size, cut, products):
    return pl.CostEstimate(
        flops=2 * size * size * (cut + products * size),
        bytes_accessed=8 * size * cut + 8 * size * size,
        transcendentals=0,
    )


def prune_first(own, other, error, down, kept, cut):
    size = own.shape[0]
    half = pl.BlockSpec((size, cut), lambda i: (0, 0))
    square = whole((size, size))
    return pl.pallas_call(
        prune_kernel,
        out_shape=[
            jax.ShapeDtypeStruct((size, cut), BF),
            jax.ShapeDtypeStruct((size, size), BF),
        ],
        grid=(1,),
        in_specs=[square, square, half, half, half],
        out_specs=[half, square],
        compiler_params=params("arbitrary"),
        cost_estimate=prune_cost(size, cut, 6),
        name="prune",
    )(own, other, error, down, kept)


def prune_next(inverse, error, down, kept, cut, at):
    size = inverse.shape[0]
    half = pl.BlockSpec((size, cut), lambda i: (0, at))
    return pl.pallas_call(
        correct_kernel,
        out_shape=jax.ShapeDtypeStruct((size, cut), BF),
        grid=(1,),
        in_specs=[whole((size, size)), half, half, half],
        out_specs=whole((size, cut)),
        compiler_params=params("arbitrary"),
        cost_estimate=prune_cost(size, cut, 0),
        name="prune_next",
    )(inverse, error, down, kept)


def stage_kernel(*refs):
    count = len(refs) // 2
    for given, out in zip(refs[:count], refs[count:]):
        out[...] = given[...]


def stage(arrays):
    rows, width = arrays[0].shape
    spec = pl.BlockSpec((CHUNK, width), lambda i: (i, 0))
    return pl.pallas_call(
        stage_kernel,
        out_shape=[jax.ShapeDtypeStruct(a.shape, a.dtype) for a in arrays],
        grid=(rows // CHUNK,),
        in_specs=[spec] * len(arrays),
        out_specs=[spec] * len(arrays),
        compiler_params=params("arbitrary"),
        name="stage",
    )(*arrays)


def tied(values):
    return lax.optimization_barrier(values)


def outputs_kernel(block, arrived, own_hidden, other_hidden, own_ref, other_ref, *refs):
    total = dot(own_hidden[...], own_ref[...]) + dot(other_hidden[...], other_ref[...])
    first, second = total[:block], total[block:]
    if arrived:
        size = refs[0].shape[0]
        from_right, from_left = refs[0][...].astype(F32), refs[1][...].astype(F32)
        if size < block:
            empty = jnp.zeros((block - size, total.shape[1]), F32)
            from_left = jnp.concatenate([from_left, empty], axis=0)
            from_right = jnp.concatenate([empty, from_right], axis=0)
        first, second = first + from_right, second + from_left
    refs[-2][...] = first.astype(BF)
    refs[-1][...] = second.astype(BF)


def column_specs(hidden, rows, ff):
    return [pl.BlockSpec((rows, ff), lambda i, at=at: (0, at)) for _, at in hidden]


def outputs(hidden, own, other, arrived):
    rows = hidden[0][0].shape[0]
    ff, cut = own.shape
    given = (hidden[0][0], hidden[1][0], own, other) + arrived
    return pl.pallas_call(
        functools.partial(outputs_kernel, rows // 2, len(arrived)),
        out_shape=[jax.ShapeDtypeStruct((rows // 2, cut), BF)] * 2,
        grid=(1,),
        in_specs=column_specs(hidden, rows, ff) + [whole(g.shape) for g in given[2:]],
        out_specs=[whole((rows // 2, cut))] * 2,
        compiler_params=params("arbitrary"),
        cost_estimate=pl.CostEstimate(
            flops=4 * rows * own.shape[0] * cut,
            bytes_accessed=sum(g.size * 2 for g in given) + rows * cut * 2,
            transcendentals=0,
        ),
        name="outputs",
    )(*given)


def self_kernel(own_hidden, other_hidden, own_ref, other_ref, out_ref):
    out_ref[...] = dot(own_hidden[...], own_ref[...]) + dot(other_hidden[...], other_ref[...])


def self_outputs(hidden, own, other):
    rows, ff, cut = hidden[0][0].shape[0], *own.shape
    given = (hidden[0][0], hidden[1][0], own, other)
    return pl.pallas_call(
        self_kernel,
        out_shape=jax.ShapeDtypeStruct((rows, cut), F32),
        grid=(1,),
        in_specs=column_specs(hidden, rows, ff) + [whole(own.shape)] * 2,
        out_specs=whole((rows, cut)),
        compiler_params=params("arbitrary"),
        name="self_outputs",
    )(*given)


def finish_kernel(own_ref, right_ref, left_ref, *refs):
    total = own_ref[...] + right_ref[...].astype(F32) + left_ref[...].astype(F32)
    refs[-1][...] = total.astype(BF)


def finish(own, right, left, width, at, result):
    rows, cut = own.shape
    given = (own, right, left) + (() if result is None else (result,))
    return pl.pallas_call(
        finish_kernel,
        out_shape=jax.ShapeDtypeStruct((rows, width), BF),
        grid=(1,),
        in_specs=[whole((rows, cut))] * 3
        + ([] if result is None else [pl.BlockSpec(memory_space=pl.ANY)]),
        out_specs=pl.BlockSpec((rows, cut), lambda i: (0, at)),
        input_output_aliases={} if result is None else {3: 0},
        compiler_params=params("arbitrary"),
        name="finish",
    )(*given)


def ring_of(expert_size, mp_size):
    chips = mp_size // 2
    order = [(z, 0) for z in range(expert_size)]
    for z in reversed(range(expert_size)):
        side = list(range(1, chips)) if (expert_size - 1 - z) % 2 == 0 else list(range(chips - 1, 0, -1))
        order += [(z, x) for x in side]
    return [z * mp_size + 2 * x for z, x in order]


def dense(expert_size, mp_size, tokens, expert_ids, route_weights, gate, up, down, code):
    gate, up, down, code = gate[0], up[0], down[0], code[0]
    tok_rows, width = tokens.shape
    devices = expert_size * mp_size
    ring = ring_of(expert_size, mp_size)
    length = len(ring)
    reach = length // 2
    here = lax.axis_index(AXES)

    def shift(value, by):
        pairs = [
            (ring[i] + c, ring[(i + by) % length] + c) for i in range(length) for c in range(2)
        ]
        return lax.ppermute(value, AXES, pairs)

    def swap(value):
        return lax.ppermute(value, AXES, [(i, i ^ 1) for i in range(devices)])

    place = jnp.stack([here, here ^ 1]).astype(jnp.int32)
    top_wide, bottom_wide, bottom, top = split(tokens, expert_ids, route_weights, devices)
    right, left = [top_wide, bottom], [top, bottom_wide]
    groups = [((top_wide, bottom), (0,))]

    def hop_first(hop):
        right[0], left[1] = shift(right[0], 1), shift(left[1], -1)
        if hop == reach:
            groups.append(((right[0], left[1]), (0,)))

    def hop_second(hop):
        right[1], left[0] = shift(right[1], 1), shift(left[0], -1)
        groups.append(((*right, *left), (0, 3)))

    pairs = [(gate, up), (swap(gate), swap(up))]
    grams = []
    hidden = []

    def work(hop):
        value, *after = hidden_part(place, (0, 1), devices, *groups[hop], pairs, grams)
        grams[:] = after
        hidden.append(((value, 0), (value, 1)))

    hop_first(1)
    kept, error = masks(code, down)
    right[1], left[0], kept, error = tied((right[1], left[0], kept, error))
    hop_second(1)
    hop_first(2)
    pairs[1] = stage(pairs[1])
    work(0)
    right[1], left[0], *grams = tied((right[1], left[0], *grams))
    hop_second(2)
    for hop in range(3, reach + 1):
        work(hop - 2)
        right[0], left[1], *grams = tied((right[0], left[1], *grams))
        hop_first(hop)
        if hop < reach:
            hop_second(hop)
    work(reach - 1)
    grams = list(tied(tuple(grams)))
    last_other, gram_other = hidden_part(
        place, (1,), devices, *groups[reach], pairs[1:], grams[1:]
    )
    gram_other = swap(gram_other)
    last_own, gram_own = hidden_part(place, (0,), devices, *groups[reach], pairs[:1], grams[:1])
    hidden.append(((last_own, 0), (last_other, 0)))
    cut = width // 2
    pruned = [None, None]
    pruned[0], inverse = prune_first(gram_own, gram_other, error, down, kept, cut)
    pruned_other = [swap(pruned[0]), None]
    pruned[1] = prune_next(inverse, error, down, kept, cut, 1)
    pruned_other[1] = swap(pruned[1])

    moving = [(), ()]
    for hop in range(reach, 0, -1):
        for at in range(2):
            sent = outputs(hidden[hop], pruned[at], pruned_other[at], moving[at])
            go_left, go_right = sent if hop < reach else (sent[1], sent[0])
            moving[at] = (shift(go_left, -1), shift(go_right, 1))
    mixed = None
    for at in range(2):
        own = self_outputs(hidden[0], pruned[at], pruned_other[at])
        mixed = finish(own, *moving[at], width, at, mixed)
    return mixed, jnp.concatenate(pruned, axis=1)[None]


def local(expert_size, mp_size, section_size, *given):
    tokens, expert_ids, _, gate_weight = given[:4]
    devices = expert_size * mp_size
    if (
        section_size == 1
        and gate_weight.shape[0] == 1
        and 2 * expert_ids.shape[1] >= devices
        and mp_size % 2 == 0
        and devices >= 16
        and devices % EXTRA == 0
        and expert_ids.shape[0] == 128
        and 2 * devices * 128 <= EXTRA * tokens.shape[1]
    ):
        return dense(expert_size, mp_size, *given)
    return routed(*given)


def solution(mesh):
    placed = (
        P(("groups", "expert", "mp"), "section"),
        P(("groups", "expert", "mp"), None),
        P(("groups", "expert", "mp"), None),
        P(("expert", "mp"), "section", None),
        P(("expert", "mp"), "section", None),
        P(("expert", "mp"), None, "section"),
        P(("expert", "mp"), None, "section"),
    )
    sizes = mesh.shape
    return jax.shard_map(
        functools.partial(local, sizes["expert"], sizes["mp"], sizes["section"]),
        mesh=mesh,
        in_specs=placed,
        out_specs=(
            P(("groups", "expert", "mp"), "section"),
            P(("groups", "expert", "mp"), None, "section"),
        ),
        check_vma=False,
    )
```

```python
import functools
import jax
import jax.numpy as jnp
import numpy as np
from jax import lax
from jax.experimental import pallas as pl
from jax.experimental.pallas import tpu as pltpu
from jax.sharding import PartitionSpec as P

FF = 384
NS = 4


DAMPING = 0.01
EPSILON = 1e-06


def decode(mask_code):
    first_row = (mask_code <= 2).astype(jnp.float32)
    second_row = ((mask_code == 0) | (mask_code == 3) | (mask_code == 4)).astype(jnp.float32)
    third_row = ((mask_code == 1) | (mask_code == 3) | (mask_code == 5)).astype(jnp.float32)
    fourth_row = ((mask_code == 2) | (mask_code == 4) | (mask_code == 5)).astype(jnp.float32)
    kept_mask = jnp.stack([first_row, second_row, third_row, fourth_row], axis=2)
    return kept_mask.reshape(mask_code.shape[0], mask_code.shape[1] * 4, mask_code.shape[2])


def precise_matmul(left, right):
    return jnp.einsum(
        "jab,jbc->jac",
        left,
        right,
        precision=lax.Precision.HIGHEST,
        preferred_element_type=jnp.float32,
    )


def routed(tokens, expert_ids, route_weights, gate_weight, up_weight, down_weight, mask_code):
    group_count = lax.axis_size(("expert", "mp"))
    experts_here, half_rows, model_width = gate_weight.shape
    tok_rows, top_count = expert_ids.shape
    experts_all = experts_here * group_count
    capacity = min(tok_rows, 5 * tok_rows * top_count // (4 * experts_all))
    slot_total = group_count * capacity
    flat_ids = expert_ids.reshape(-1)
    onehot = (flat_ids[:, None] == jnp.arange(experts_all, dtype=jnp.int32)[None, :]).astype(
        jnp.int32
    )
    slot_rank = jnp.sum((jnp.cumsum(onehot, axis=0) - onehot) * onehot, axis=1)
    local_expert = flat_ids % experts_here
    position = flat_ids // experts_here * capacity + slot_rank
    token_of = jnp.arange(tok_rows * top_count, dtype=jnp.int32) // top_count
    slot_token = (
        jnp.full((experts_here, slot_total), tok_rows, jnp.int32)
        .at[local_expert, position]
        .set(token_of)
    )
    full_rows = lax.all_gather(tokens, "section", axis=1, tiled=True)
    padded_rows = jnp.concatenate(
        [full_rows, jnp.zeros((1, full_rows.shape[1]), full_rows.dtype)], axis=0
    )
    send_rows = padded_rows[slot_token]
    slot_rows = lax.all_to_all(send_rows, ("expert", "mp"), split_axis=1, concat_axis=1, tiled=True)
    gate_pre = jnp.einsum(
        "jfd,jsd->jfs", gate_weight, slot_rows, preferred_element_type=jnp.float32
    )
    up_pre = jnp.einsum("jfd,jsd->jfs", up_weight, slot_rows, preferred_element_type=jnp.float32)
    hidden_half = (jax.nn.silu(gate_pre) * up_pre).astype(jnp.bfloat16)
    hidden_all = lax.all_gather(hidden_half, "section", axis=1, tiled=True)
    hidden_width = hidden_all.shape[1]
    gram_matrix = jnp.einsum(
        "jfs,jgs->jfg", hidden_all, hidden_all, preferred_element_type=jnp.float32
    )
    mean_diag = jnp.mean(jnp.diagonal(gram_matrix, axis1=1, axis2=2), axis=1)
    identity = jnp.eye(hidden_width, dtype=jnp.float32)
    hessian = gram_matrix + (DAMPING * mean_diag + EPSILON)[:, None, None] * identity
    step_size = 1.0 / jnp.max(jnp.sum(jnp.abs(hessian), axis=2), axis=1)
    iterate = (
        2.0 * step_size[:, None, None] * identity - (step_size * step_size)[:, None, None] * hessian
    )
    for iteration in range(NS - 1):
        iterate = 2.0 * iterate - precise_matmul(precise_matmul(iterate, hessian), iterate)
    kept_mask = decode(mask_code)
    weight_wide = down_weight.astype(jnp.float32)
    inverse_diag = jnp.diagonal(iterate, axis1=1, axis2=2)
    scaled_error = weight_wide * (1.0 - kept_mask) / inverse_diag[:, :, None]
    correction = precise_matmul(iterate, scaled_error)
    pruned = (kept_mask * (weight_wide - correction)).astype(jnp.bfloat16)
    expert_out = (
        jnp.einsum("jfs,jfd->jsd", hidden_all, pruned, preferred_element_type=jnp.float32)
        * FF ** (-0.5)
    ).astype(jnp.bfloat16)
    returned = lax.all_to_all(expert_out, ("expert", "mp"), split_axis=1, concat_axis=1, tiled=True)
    picked = returned[local_expert, position].reshape(tok_rows, top_count, -1)
    combined = jnp.einsum("tkd,tk->td", picked.astype(jnp.float32), route_weights)
    return (combined.astype(jnp.bfloat16), pruned)


AXES = ("expert", "mp")
CHUNK = 128
EXTRA = 8
BF = jnp.bfloat16
F32 = jnp.float32


def params(*semantics, mib=16):
    return pltpu.CompilerParams(
        dimension_semantics=semantics or None, vmem_limit_bytes=mib * 1024 * 1024
    )


def whole(shape):
    return pl.BlockSpec(shape, lambda *_: (0,) * len(shape))


def dot(left, right, on=((1,), (0,))):
    return lax.dot_general(left, right, (on, ((), ())), preferred_element_type=F32)


def split_kernel(experts_all, x_ref, ids_ref, weight_ref, *out_refs):
    half = x_ref.shape[0] // 2
    ids, weight = ids_ref[...], weight_ref[...]
    table = [
        jnp.max(jnp.where(ids == e, weight, -1.0), axis=0, keepdims=True)
        for e in range(experts_all)
    ]
    table = jnp.concatenate(table, axis=0)
    high = table.astype(BF).astype(F32)
    both = jnp.concatenate([high, table - high], axis=0)
    parts = [both[i : i + EXTRA] for i in range(0, 2 * experts_all, EXTRA)]
    lanes = both.shape[1]
    rest = x_ref.shape[1] - len(parts) * lanes
    extra = jnp.concatenate(parts + [jnp.zeros((EXTRA, rest), F32)], axis=1).astype(BF)
    for at, (wide, plain) in enumerate(((out_refs[0], out_refs[3]), (out_refs[1], out_refs[2]))):
        value = x_ref[at * half : (at + 1) * half, :]
        wide[:half, :] = value
        wide[half:, :] = extra
        plain[...] = value


def split(tokens, expert_ids, route_weights, experts_all):
    rows, width = tokens.shape
    wide = jax.ShapeDtypeStruct((rows // 2 + EXTRA, width), BF)
    plain = jax.ShapeDtypeStruct((rows // 2, width), BF)
    given = (tokens, expert_ids.T, route_weights.T)
    return pl.pallas_call(
        functools.partial(split_kernel, experts_all),
        out_shape=[wide, wide, plain, plain],
        grid=(1,),
        in_specs=[whole(g.shape) for g in given],
        out_specs=[whole(o.shape) for o in (wide, wide, plain, plain)],
        compiler_params=params("arbitrary", mib=56),
        name="split",
    )(*given)


def token_weights(ref, experts_all, expert):
    half, lanes = ref.shape[0] - EXTRA, 2 * (ref.shape[0] - EXTRA)
    count = 2 * experts_all // EXTRA
    parts = [ref[half:, i * lanes : (i + 1) * lanes].astype(F32) for i in range(count)]
    both = jnp.concatenate(parts, axis=0)
    table = both[:experts_all] + both[experts_all:]
    row = lax.broadcasted_iota(jnp.int32, table.shape, 0)
    return jnp.sum(jnp.where(row == expert, table, 0.0), axis=0, keepdims=True)


def mask_kernel(code_ref, down_ref, kept_ref, error_ref):
    rows, groups = down_ref.shape[0], code_ref.shape[0]
    code = code_ref[...]
    first = code <= 2
    second = (code == 0) | (code == 3) | (code == 4)
    third = (code == 1) | (code == 3) | (code == 5)
    fourth = (code == 2) | (code == 4) | (code == 5)
    planes = [jnp.where(plane, 1.0, 0.0).astype(BF) for plane in (first, second, third, fourth)]
    row = lax.broadcasted_iota(jnp.int32, (rows, rows), 0)
    column = lax.broadcasted_iota(jnp.int32, (rows, rows), 1)
    spread = jnp.where(row % 4 * groups + row // 4 == column, 1.0, 0.0).astype(BF)
    kept = dot(spread, jnp.concatenate(planes, axis=0))
    kept_ref[...] = kept.astype(BF)
    error_ref[...] = jnp.where(kept > 0.5, 0.0, down_ref[...].astype(F32)).astype(BF)


def masks(code, down):
    groups, width = code.shape
    rows = down.shape[0]
    cut = 512
    spec = pl.BlockSpec((rows, cut), lambda i: (0, i))
    return pl.pallas_call(
        mask_kernel,
        out_shape=[jax.ShapeDtypeStruct((rows, width), BF)] * 2,
        grid=(width // cut,),
        in_specs=[pl.BlockSpec((groups, cut), lambda i: (0, i)), spec],
        out_specs=[spec, spec],
        compiler_params=params("arbitrary"),
        cost_estimate=pl.CostEstimate(
            flops=2 * rows * rows * width, bytes_accessed=8 * rows * width, transcendentals=0
        ),
        name="masks",
    )(code, down)


def hidden_kernel(pieces, sources, experts, experts_all, has_gram, place_ref, *refs):
    count = len(experts)
    x_refs, refs = refs[:pieces], refs[pieces:]
    pairs, grams_in = refs[: 2 * count], refs[2 * count : 3 * count]
    out_ref, gram_refs, rows_ref = refs[-2 - count], refs[-1 - count : -1], refs[-1]
    half = min(x.shape[0] for x in x_refs)
    half = half - half % 16
    for at, x in enumerate(x_refs):
        rows_ref[at * half : (at + 1) * half, :] = x[:half, :]
    for which in range(count):
        gate_ref, up_ref = pairs[2 * which], pairs[2 * which + 1]
        ff = gate_ref.shape[0]
        weight = [
            token_weights(x_refs[i], experts_all, place_ref[experts[which]]) for i in sources
        ]
        empty = jnp.zeros((8 - len(sources), weight[0].shape[1]), F32)
        weight = jnp.concatenate(weight + [empty], axis=0).T
        weight = jnp.concatenate([weight[:, at : at + 1] for at in range(len(sources))], axis=0)
        parts = []
        for at in range(0, ff, CHUNK):
            both = [gate_ref[at : at + CHUNK, :], up_ref[at : at + CHUNK, :]]
            pre = dot(rows_ref[...], jnp.concatenate(both, axis=0), ((1,), (1,)))
            gate, up = pre[:, :CHUNK], pre[:, CHUNK:]
            value = gate / (1.0 + jnp.exp(-gate)) * up
            value = jnp.where(weight >= 0.0, value, 0.0).astype(BF)
            column = which * ff + at
            out_ref[:, column : column + CHUNK] = (
                value.astype(F32) * (weight * FF ** (-0.5))
            ).astype(BF)
            parts.append(value)
        hidden = jnp.concatenate(parts, axis=1)
        gram = dot(hidden, hidden, ((0,), (0,)))
        gram_refs[which][...] = grams_in[which][...] + gram if has_gram else gram


def hidden_part(place, experts, experts_all, pieces, sources, pairs, grams):
    half = min(p.shape[0] for p in pieces)
    rows = len(pieces) * (half - half % 16)
    ff, width = pairs[0][0].shape
    count = len(experts)
    resident = pl.BlockSpec(memory_space=pltpu.VMEM)
    given = [*pieces] + [w for pair in pairs for w in pair] + [*grams]
    return pl.pallas_call(
        functools.partial(
            hidden_kernel, len(pieces), sources, experts, experts_all, len(grams) > 0
        ),
        out_shape=[jax.ShapeDtypeStruct((rows, count * ff), BF)]
        + [jax.ShapeDtypeStruct((ff, ff), F32)] * count,
        in_specs=[pl.BlockSpec(memory_space=pltpu.SMEM)] + [resident] * len(given),
        out_specs=[resident] * (1 + count),
        scratch_shapes=[pltpu.VMEM((rows, width), BF)],
        compiler_params=params(),
        cost_estimate=pl.CostEstimate(
            flops=4 * rows * ff * width * count,
            bytes_accessed=2 * (rows + 2 * ff * count) * width,
            transcendentals=rows * ff * count,
        ),
        name="hidden",
    )(place, *given)


def product(left, right):
    return dot(left.astype(BF), right)


def prune_kernel(own_ref, other_ref, error_ref, down_ref, kept_ref, out_ref, inverse_ref):
    gram = own_ref[...] + other_ref[...]
    size = gram.shape[0]
    row = lax.broadcasted_iota(jnp.int32, (size, size), 0)
    column = lax.broadcasted_iota(jnp.int32, (size, size), 1)
    eye = row == column
    mean_diag = jnp.sum(jnp.where(eye, gram, 0.0)) * (1.0 / size)
    hessian = gram + jnp.where(eye, DAMPING * mean_diag + EPSILON, 0.0)
    step_size = 1.0 / jnp.max(jnp.sum(jnp.abs(hessian), axis=0, keepdims=True))
    scaled = step_size * hessian
    iterate = jnp.where(eye, 2.0, 0.0) - scaled
    right = scaled.astype(BF)
    scaled = 2.0 * scaled - dot(right, right)
    for iteration in range(NS - 1):
        right = scaled.astype(BF)
        following = 2.0 * iterate - product(iterate, right)
        if iteration < NS - 2:
            scaled = 2.0 * scaled - dot(right, right)
        iterate = following
    diag = jnp.sum(jnp.where(eye, iterate, 0.0), axis=0, keepdims=True)
    inverse_ref[...] = (iterate * (1.0 / diag)).astype(BF)
    correct_kernel(inverse_ref, error_ref, down_ref, kept_ref, out_ref)


def correct_kernel(inverse_ref, error_ref, down_ref, kept_ref, out_ref):
    correction = dot(inverse_ref[...], error_ref[...])
    value = kept_ref[...].astype(F32) * (down_ref[...].astype(F32) - correction)
    out_ref[...] = value.astype(BF)


def prune_cost(size, cut, products):
    return pl.CostEstimate(
        flops=2 * size * size * (cut + products * size),
        bytes_accessed=8 * size * cut + 8 * size * size,
        transcendentals=0,
    )


def prune_first(own, other, error, down, kept, cut):
    size = own.shape[0]
    half = pl.BlockSpec((size, cut), lambda i: (0, 0))
    square = whole((size, size))
    return pl.pallas_call(
        prune_kernel,
        out_shape=[
            jax.ShapeDtypeStruct((size, cut), BF),
            jax.ShapeDtypeStruct((size, size), BF),
        ],
        grid=(1,),
        in_specs=[square, square, half, half, half],
        out_specs=[half, square],
        compiler_params=params("arbitrary"),
        cost_estimate=prune_cost(size, cut, 6),
        name="prune",
    )(own, other, error, down, kept)


def prune_next(inverse, error, down, kept, cut, at):
    size = inverse.shape[0]
    half = pl.BlockSpec((size, cut), lambda i: (0, at))
    return pl.pallas_call(
        correct_kernel,
        out_shape=jax.ShapeDtypeStruct((size, cut), BF),
        grid=(1,),
        in_specs=[whole((size, size)), half, half, half],
        out_specs=whole((size, cut)),
        compiler_params=params("arbitrary"),
        cost_estimate=prune_cost(size, cut, 0),
        name="prune_next",
    )(inverse, error, down, kept)


def stage_kernel(*refs):
    count = len(refs) // 2
    for given, out in zip(refs[:count], refs[count:]):
        out[...] = given[...]


def stage(arrays):
    rows, width = arrays[0].shape
    spec = pl.BlockSpec((CHUNK, width), lambda i: (i, 0))
    return pl.pallas_call(
        stage_kernel,
        out_shape=[jax.ShapeDtypeStruct(a.shape, a.dtype) for a in arrays],
        grid=(rows // CHUNK,),
        in_specs=[spec] * len(arrays),
        out_specs=[spec] * len(arrays),
        compiler_params=params("arbitrary"),
        name="stage",
    )(*arrays)


def tied(values):
    return lax.optimization_barrier(values)


def outputs_kernel(block, arrived, own_hidden, other_hidden, own_ref, other_ref, *refs):
    total = dot(own_hidden[...], own_ref[...]) + dot(other_hidden[...], other_ref[...])
    first, second = total[:block], total[block:]
    if arrived:
        size = refs[0].shape[0]
        from_right, from_left = refs[0][...].astype(F32), refs[1][...].astype(F32)
        if size < block:
            empty = jnp.zeros((block - size, total.shape[1]), F32)
            from_left = jnp.concatenate([from_left, empty], axis=0)
            from_right = jnp.concatenate([empty, from_right], axis=0)
        first, second = first + from_right, second + from_left
    refs[-2][...] = first.astype(BF)
    refs[-1][...] = second.astype(BF)


def column_specs(hidden, rows, ff):
    return [pl.BlockSpec((rows, ff), lambda i, at=at: (0, at)) for _, at in hidden]


def outputs(hidden, own, other, arrived):
    rows = hidden[0][0].shape[0]
    ff, cut = own.shape
    given = (hidden[0][0], hidden[1][0], own, other) + arrived
    return pl.pallas_call(
        functools.partial(outputs_kernel, rows // 2, len(arrived)),
        out_shape=[jax.ShapeDtypeStruct((rows // 2, cut), BF)] * 2,
        grid=(1,),
        in_specs=column_specs(hidden, rows, ff) + [whole(g.shape) for g in given[2:]],
        out_specs=[whole((rows // 2, cut))] * 2,
        compiler_params=params("arbitrary"),
        cost_estimate=pl.CostEstimate(
            flops=4 * rows * own.shape[0] * cut,
            bytes_accessed=sum(g.size * 2 for g in given) + rows * cut * 2,
            transcendentals=0,
        ),
        name="outputs",
    )(*given)


def self_kernel(own_hidden, other_hidden, own_ref, other_ref, out_ref):
    out_ref[...] = dot(own_hidden[...], own_ref[...]) + dot(other_hidden[...], other_ref[...])


def self_outputs(hidden, own, other):
    rows, ff, cut = hidden[0][0].shape[0], *own.shape
    given = (hidden[0][0], hidden[1][0], own, other)
    return pl.pallas_call(
        self_kernel,
        out_shape=jax.ShapeDtypeStruct((rows, cut), F32),
        grid=(1,),
        in_specs=column_specs(hidden, rows, ff) + [whole(own.shape)] * 2,
        out_specs=whole((rows, cut)),
        compiler_params=params("arbitrary"),
        name="self_outputs",
    )(*given)


def finish_kernel(own_ref, right_ref, left_ref, *refs):
    total = own_ref[...] + right_ref[...].astype(F32) + left_ref[...].astype(F32)
    refs[-1][...] = total.astype(BF)


def finish(own, right, left, width, at, result):
    rows, cut = own.shape
    given = (own, right, left) + (() if result is None else (result,))
    return pl.pallas_call(
        finish_kernel,
        out_shape=jax.ShapeDtypeStruct((rows, width), BF),
        grid=(1,),
        in_specs=[whole((rows, cut))] * 3
        + ([] if result is None else [pl.BlockSpec(memory_space=pl.ANY)]),
        out_specs=pl.BlockSpec((rows, cut), lambda i: (0, at)),
        input_output_aliases={} if result is None else {3: 0},
        compiler_params=params("arbitrary"),
        name="finish",
    )(*given)


def ring_of(expert_size, mp_size):
    chips = mp_size // 2
    order = [(z, 0) for z in range(expert_size)]
    for z in reversed(range(expert_size)):
        side = list(range(1, chips)) if (expert_size - 1 - z) % 2 == 0 else list(range(chips - 1, 0, -1))
        order += [(z, x) for x in side]
    return [z * mp_size + 2 * x for z, x in order]


def dense(expert_size, mp_size, tokens, expert_ids, route_weights, gate, up, down, code):
    gate, up, down, code = gate[0], up[0], down[0], code[0]
    tok_rows, width = tokens.shape
    devices = expert_size * mp_size
    ring = ring_of(expert_size, mp_size)
    length = len(ring)
    reach = length // 2
    here = lax.axis_index(AXES)

    def shift(value, by):
        pairs = [
            (ring[i] + c, ring[(i + by) % length] + c) for i in range(length) for c in range(2)
        ]
        return lax.ppermute(value, AXES, pairs)

    def swap(value):
        return lax.ppermute(value, AXES, [(i, i ^ 1) for i in range(devices)])

    place = jnp.stack([here, here ^ 1]).astype(jnp.int32)
    top_wide, bottom_wide, bottom, top = split(tokens, expert_ids, route_weights, devices)

    def hop_first(hop):
        right[0], left[1] = shift(right[0], 1), shift(left[1], -1)
        if hop == reach:
            groups.append(((right[0], left[1]), (0,)))

    def hop_second(hop):
        right[1], left[0] = shift(right[1], 1), shift(left[0], -1)
        groups.append(((*right, *left), (0, 3)))

    top_wide, bottom_wide, gate_sent, up_sent = tied((top_wide, bottom_wide, gate, up))
    pairs = [(gate, up), (swap(gate_sent), swap(up_sent))]
    right, left = [top_wide, bottom], [top, bottom_wide]
    groups = [((top_wide, bottom), (0,))]
    grams = []
    hidden = []

    def work(hop):
        value, *after = hidden_part(place, (0, 1), devices, *groups[hop], pairs, grams)
        grams[:] = after
        hidden.append(((value, 0), (value, 1)))

    hop_first(1)
    kept, error = masks(code, down)
    right[1], left[0], kept, error = tied((right[1], left[0], kept, error))
    hop_second(1)
    hop_first(2)
    pairs[1] = stage(pairs[1])
    work(0)
    right[1], left[0], *grams = tied((right[1], left[0], *grams))
    hop_second(2)
    for hop in range(3, reach + 1):
        work(hop - 2)
        right[0], left[1], *grams = tied((right[0], left[1], *grams))
        hop_first(hop)
        if hop < reach:
            hop_second(hop)
    work(reach - 1)
    grams = list(tied(tuple(grams)))
    last_other, gram_other = hidden_part(
        place, (1,), devices, *groups[reach], pairs[1:], grams[1:]
    )
    gram_other = swap(gram_other)
    last_own, gram_own = hidden_part(place, (0,), devices, *groups[reach], pairs[:1], grams[:1])
    hidden.append(((last_own, 0), (last_other, 0)))
    cut = width // 2
    pruned = [None, None]
    pruned[0], inverse = prune_first(gram_own, gram_other, error, down, kept, cut)
    pruned_other = [swap(pruned[0]), None]
    pruned[1] = prune_next(inverse, error, down, kept, cut, 1)
    pruned_other[1] = swap(pruned[1])

    moving = [(), ()]
    for hop in range(reach, 0, -1):
        for at in range(2):
            sent = outputs(hidden[hop], pruned[at], pruned_other[at], moving[at])
            go_left, go_right = sent if hop < reach else (sent[1], sent[0])
            moving[at] = (shift(go_left, -1), shift(go_right, 1))
    mixed = None
    for at in range(2):
        own = self_outputs(hidden[0], pruned[at], pruned_other[at])
        mixed = finish(own, *moving[at], width, at, mixed)
    return mixed, jnp.concatenate(pruned, axis=1)[None]


def local(expert_size, mp_size, section_size, *given):
    tokens, expert_ids, _, gate_weight = given[:4]
    devices = expert_size * mp_size
    if (
        section_size == 1
        and gate_weight.shape[0] == 1
        and 2 * expert_ids.shape[1] >= devices
        and mp_size % 2 == 0
        and devices >= 16
        and devices % EXTRA == 0
        and expert_ids.shape[0] == 128
        and 2 * devices * 128 <= EXTRA * tokens.shape[1]
    ):
        return dense(expert_size, mp_size, *given)
    return routed(*given)


def solution(mesh):
    placed = (
        P(("groups", "expert", "mp"), "section"),
        P(("groups", "expert", "mp"), None),
        P(("groups", "expert", "mp"), None),
        P(("expert", "mp"), "section", None),
        P(("expert", "mp"), "section", None),
        P(("expert", "mp"), None, "section"),
        P(("expert", "mp"), None, "section"),
    )
    sizes = mesh.shape
    return jax.shard_map(
        functools.partial(local, sizes["expert"], sizes["mp"], sizes["section"]),
        mesh=mesh,
        in_specs=placed,
        out_specs=(
            P(("groups", "expert", "mp"), "section"),
            P(("groups", "expert", "mp"), None, "section"),
        ),
        check_vma=False,
    )
```

```python
import functools
import jax
import jax.numpy as jnp
import numpy as np
from jax import lax
from jax.experimental import pallas as pl
from jax.experimental.pallas import tpu as pltpu
from jax.sharding import PartitionSpec as P

FF = 384
NS = 4


DAMPING = 0.01
EPSILON = 1e-06


def decode(mask_code):
    first_row = (mask_code <= 2).astype(jnp.float32)
    second_row = ((mask_code == 0) | (mask_code == 3) | (mask_code == 4)).astype(jnp.float32)
    third_row = ((mask_code == 1) | (mask_code == 3) | (mask_code == 5)).astype(jnp.float32)
    fourth_row = ((mask_code == 2) | (mask_code == 4) | (mask_code == 5)).astype(jnp.float32)
    kept_mask = jnp.stack([first_row, second_row, third_row, fourth_row], axis=2)
    return kept_mask.reshape(mask_code.shape[0], mask_code.shape[1] * 4, mask_code.shape[2])


def precise_matmul(left, right):
    return jnp.einsum(
        "jab,jbc->jac",
        left,
        right,
        precision=lax.Precision.HIGHEST,
        preferred_element_type=jnp.float32,
    )


def routed(tokens, expert_ids, route_weights, gate_weight, up_weight, down_weight, mask_code):
    group_count = lax.axis_size(("expert", "mp"))
    experts_here, half_rows, model_width = gate_weight.shape
    tok_rows, top_count = expert_ids.shape
    experts_all = experts_here * group_count
    capacity = min(tok_rows, 5 * tok_rows * top_count // (4 * experts_all))
    slot_total = group_count * capacity
    flat_ids = expert_ids.reshape(-1)
    onehot = (flat_ids[:, None] == jnp.arange(experts_all, dtype=jnp.int32)[None, :]).astype(
        jnp.int32
    )
    slot_rank = jnp.sum((jnp.cumsum(onehot, axis=0) - onehot) * onehot, axis=1)
    local_expert = flat_ids % experts_here
    position = flat_ids // experts_here * capacity + slot_rank
    token_of = jnp.arange(tok_rows * top_count, dtype=jnp.int32) // top_count
    slot_token = (
        jnp.full((experts_here, slot_total), tok_rows, jnp.int32)
        .at[local_expert, position]
        .set(token_of)
    )
    full_rows = lax.all_gather(tokens, "section", axis=1, tiled=True)
    padded_rows = jnp.concatenate(
        [full_rows, jnp.zeros((1, full_rows.shape[1]), full_rows.dtype)], axis=0
    )
    send_rows = padded_rows[slot_token]
    slot_rows = lax.all_to_all(send_rows, ("expert", "mp"), split_axis=1, concat_axis=1, tiled=True)
    gate_pre = jnp.einsum(
        "jfd,jsd->jfs", gate_weight, slot_rows, preferred_element_type=jnp.float32
    )
    up_pre = jnp.einsum("jfd,jsd->jfs", up_weight, slot_rows, preferred_element_type=jnp.float32)
    hidden_half = (jax.nn.silu(gate_pre) * up_pre).astype(jnp.bfloat16)
    hidden_all = lax.all_gather(hidden_half, "section", axis=1, tiled=True)
    hidden_width = hidden_all.shape[1]
    gram_matrix = jnp.einsum(
        "jfs,jgs->jfg", hidden_all, hidden_all, preferred_element_type=jnp.float32
    )
    mean_diag = jnp.mean(jnp.diagonal(gram_matrix, axis1=1, axis2=2), axis=1)
    identity = jnp.eye(hidden_width, dtype=jnp.float32)
    hessian = gram_matrix + (DAMPING * mean_diag + EPSILON)[:, None, None] * identity
    step_size = 1.0 / jnp.max(jnp.sum(jnp.abs(hessian), axis=2), axis=1)
    iterate = (
        2.0 * step_size[:, None, None] * identity - (step_size * step_size)[:, None, None] * hessian
    )
    for iteration in range(NS - 1):
        iterate = 2.0 * iterate - precise_matmul(precise_matmul(iterate, hessian), iterate)
    kept_mask = decode(mask_code)
    weight_wide = down_weight.astype(jnp.float32)
    inverse_diag = jnp.diagonal(iterate, axis1=1, axis2=2)
    scaled_error = weight_wide * (1.0 - kept_mask) / inverse_diag[:, :, None]
    correction = precise_matmul(iterate, scaled_error)
    pruned = (kept_mask * (weight_wide - correction)).astype(jnp.bfloat16)
    expert_out = (
        jnp.einsum("jfs,jfd->jsd", hidden_all, pruned, preferred_element_type=jnp.float32)
        * FF ** (-0.5)
    ).astype(jnp.bfloat16)
    returned = lax.all_to_all(expert_out, ("expert", "mp"), split_axis=1, concat_axis=1, tiled=True)
    picked = returned[local_expert, position].reshape(tok_rows, top_count, -1)
    combined = jnp.einsum("tkd,tk->td", picked.astype(jnp.float32), route_weights)
    return (combined.astype(jnp.bfloat16), pruned)


AXES = ("expert", "mp")
CHUNK = 128
EXTRA = 8
BF = jnp.bfloat16
F32 = jnp.float32


def params(*semantics, mib=16):
    return pltpu.CompilerParams(
        dimension_semantics=semantics or None, vmem_limit_bytes=mib * 1024 * 1024
    )


def whole(shape):
    return pl.BlockSpec(shape, lambda *_: (0,) * len(shape))


def dot(left, right, on=((1,), (0,))):
    return lax.dot_general(left, right, (on, ((), ())), preferred_element_type=F32)


def split_kernel(experts_all, x_ref, ids_ref, weight_ref, *out_refs):
    half = x_ref.shape[0] // 2
    ids, weight = ids_ref[...], weight_ref[...]
    table = [
        jnp.max(jnp.where(ids == e, weight, -1.0), axis=0, keepdims=True)
        for e in range(experts_all)
    ]
    table = jnp.concatenate(table, axis=0)
    high = table.astype(BF).astype(F32)
    both = jnp.concatenate([high, table - high], axis=0)
    parts = [both[i : i + EXTRA] for i in range(0, 2 * experts_all, EXTRA)]
    lanes = both.shape[1]
    rest = x_ref.shape[1] - len(parts) * lanes
    extra = jnp.concatenate(parts + [jnp.zeros((EXTRA, rest), F32)], axis=1).astype(BF)
    for at, (wide, plain) in enumerate(((out_refs[0], out_refs[3]), (out_refs[1], out_refs[2]))):
        value = x_ref[at * half : (at + 1) * half, :]
        wide[:half, :] = value
        wide[half:, :] = extra
        plain[...] = value


def split(tokens, expert_ids, route_weights, experts_all):
    rows, width = tokens.shape
    wide = jax.ShapeDtypeStruct((rows // 2 + EXTRA, width), BF)
    plain = jax.ShapeDtypeStruct((rows // 2, width), BF)
    given = (tokens, expert_ids.T, route_weights.T)
    return pl.pallas_call(
        functools.partial(split_kernel, experts_all),
        out_shape=[wide, wide, plain, plain],
        grid=(1,),
        in_specs=[whole(g.shape) for g in given],
        out_specs=[whole(o.shape) for o in (wide, wide, plain, plain)],
        compiler_params=params("arbitrary", mib=56),
        name="split",
    )(*given)


def token_weights(ref, experts_all, expert):
    half, lanes = ref.shape[0] - EXTRA, 2 * (ref.shape[0] - EXTRA)
    count = 2 * experts_all // EXTRA
    parts = [ref[half:, i * lanes : (i + 1) * lanes].astype(F32) for i in range(count)]
    both = jnp.concatenate(parts, axis=0)
    table = both[:experts_all] + both[experts_all:]
    row = lax.broadcasted_iota(jnp.int32, table.shape, 0)
    return jnp.sum(jnp.where(row == expert, table, 0.0), axis=0, keepdims=True)


def mask_kernel(code_ref, down_ref, kept_ref, error_ref):
    rows, groups = down_ref.shape[0], code_ref.shape[0]
    code = code_ref[...]
    first = code <= 2
    second = (code == 0) | (code == 3) | (code == 4)
    third = (code == 1) | (code == 3) | (code == 5)
    fourth = (code == 2) | (code == 4) | (code == 5)
    planes = [jnp.where(plane, 1.0, 0.0).astype(BF) for plane in (first, second, third, fourth)]
    row = lax.broadcasted_iota(jnp.int32, (rows, rows), 0)
    column = lax.broadcasted_iota(jnp.int32, (rows, rows), 1)
    spread = jnp.where(row % 4 * groups + row // 4 == column, 1.0, 0.0).astype(BF)
    kept = dot(spread, jnp.concatenate(planes, axis=0))
    kept_ref[...] = kept.astype(BF)
    error_ref[...] = jnp.where(kept > 0.5, 0.0, down_ref[...].astype(F32)).astype(BF)


def masks(code, down, cut, at, mib):
    groups, width = code.shape
    rows = down.shape[0]
    step = cut // 2
    first = at * 2
    taken = pl.BlockSpec((rows, step), lambda i: (0, i + first))
    given = pl.BlockSpec((rows, step), lambda i: (0, i))
    return pl.pallas_call(
        mask_kernel,
        out_shape=[jax.ShapeDtypeStruct((rows, cut), BF)] * 2,
        grid=(2,),
        in_specs=[pl.BlockSpec((groups, step), lambda i: (0, i + first)), taken],
        out_specs=[given, given],
        compiler_params=params("arbitrary", mib=mib),
        cost_estimate=pl.CostEstimate(
            flops=2 * rows * rows * cut, bytes_accessed=8 * rows * cut, transcendentals=0
        ),
        name="masks",
    )(code, down)


def hidden_kernel(pieces, sources, experts, experts_all, has_gram, place_ref, *refs):
    count = len(experts)
    x_refs, refs = refs[:pieces], refs[pieces:]
    pairs, grams_in = refs[: 2 * count], refs[2 * count : 3 * count]
    out_ref, gram_refs, rows_ref = refs[-2 - count], refs[-1 - count : -1], refs[-1]
    half = min(x.shape[0] for x in x_refs)
    half = half - half % 16
    for at, x in enumerate(x_refs):
        rows_ref[at * half : (at + 1) * half, :] = x[:half, :]
    for which in range(count):
        gate_ref, up_ref = pairs[2 * which], pairs[2 * which + 1]
        ff = gate_ref.shape[0]
        weight = [
            token_weights(x_refs[i], experts_all, place_ref[experts[which]]) for i in sources
        ]
        empty = jnp.zeros((8 - len(sources), weight[0].shape[1]), F32)
        weight = jnp.concatenate(weight + [empty], axis=0).T
        weight = jnp.concatenate([weight[:, at : at + 1] for at in range(len(sources))], axis=0)
        parts = []
        for at in range(0, ff, CHUNK):
            both = [gate_ref[at : at + CHUNK, :], up_ref[at : at + CHUNK, :]]
            pre = dot(rows_ref[...], jnp.concatenate(both, axis=0), ((1,), (1,)))
            gate, up = pre[:, :CHUNK], pre[:, CHUNK:]
            value = gate / (1.0 + jnp.exp(-gate)) * up
            value = jnp.where(weight >= 0.0, value, 0.0).astype(BF)
            column = which * ff + at
            out_ref[:, column : column + CHUNK] = (
                value.astype(F32) * (weight * FF ** (-0.5))
            ).astype(BF)
            parts.append(value)
        hidden = jnp.concatenate(parts, axis=1)
        gram = dot(hidden, hidden, ((0,), (0,)))
        gram_refs[which][...] = grams_in[which][...] + gram if has_gram else gram


def hidden_part(place, experts, experts_all, pieces, sources, pairs, grams):
    half = min(p.shape[0] for p in pieces)
    rows = len(pieces) * (half - half % 16)
    ff, width = pairs[0][0].shape
    count = len(experts)
    resident = pl.BlockSpec(memory_space=pltpu.VMEM)
    given = [*pieces] + [w for pair in pairs for w in pair] + [*grams]
    return pl.pallas_call(
        functools.partial(
            hidden_kernel, len(pieces), sources, experts, experts_all, len(grams) > 0
        ),
        out_shape=[jax.ShapeDtypeStruct((rows, count * ff), BF)]
        + [jax.ShapeDtypeStruct((ff, ff), F32)] * count,
        in_specs=[pl.BlockSpec(memory_space=pltpu.SMEM)] + [resident] * len(given),
        out_specs=[resident] * (1 + count),
        scratch_shapes=[pltpu.VMEM((rows, width), BF)],
        compiler_params=params(),
        cost_estimate=pl.CostEstimate(
            flops=4 * rows * ff * width * count,
            bytes_accessed=2 * (rows + 2 * ff * count) * width,
            transcendentals=rows * ff * count,
        ),
        name="hidden",
    )(place, *given)


def product(left, right):
    return dot(left.astype(BF), right)


def prune_kernel(own_ref, other_ref, error_ref, down_ref, kept_ref, out_ref, inverse_ref):
    gram = own_ref[...] + other_ref[...]
    size = gram.shape[0]
    row = lax.broadcasted_iota(jnp.int32, (size, size), 0)
    column = lax.broadcasted_iota(jnp.int32, (size, size), 1)
    eye = row == column
    mean_diag = jnp.sum(jnp.where(eye, gram, 0.0)) * (1.0 / size)
    hessian = gram + jnp.where(eye, DAMPING * mean_diag + EPSILON, 0.0)
    step_size = 1.0 / jnp.max(jnp.sum(jnp.abs(hessian), axis=0, keepdims=True))
    scaled = step_size * hessian
    iterate = jnp.where(eye, 2.0, 0.0) - scaled
    right = scaled.astype(BF)
    scaled = 2.0 * scaled - dot(right, right)
    for iteration in range(NS - 1):
        right = scaled.astype(BF)
        following = 2.0 * iterate - product(iterate, right)
        if iteration < NS - 2:
            scaled = 2.0 * scaled - dot(right, right)
        iterate = following
    diag = jnp.sum(jnp.where(eye, iterate, 0.0), axis=0, keepdims=True)
    inverse_ref[...] = (iterate * (1.0 / diag)).astype(BF)
    correct_kernel(inverse_ref, error_ref, down_ref, kept_ref, out_ref)


def correct_kernel(inverse_ref, error_ref, down_ref, kept_ref, out_ref):
    correction = dot(inverse_ref[...], error_ref[...])
    value = kept_ref[...].astype(F32) * (down_ref[...].astype(F32) - correction)
    out_ref[...] = value.astype(BF)


def prune_cost(size, cut, products):
    return pl.CostEstimate(
        flops=2 * size * size * (cut + products * size),
        bytes_accessed=8 * size * cut + 8 * size * size,
        transcendentals=0,
    )


def prune_first(own, other, error, down, kept, cut):
    size = own.shape[0]
    half = pl.BlockSpec((size, cut), lambda i: (0, 0))
    square = whole((size, size))
    return pl.pallas_call(
        prune_kernel,
        out_shape=[
            jax.ShapeDtypeStruct((size, cut), BF),
            jax.ShapeDtypeStruct((size, size), BF),
        ],
        grid=(1,),
        in_specs=[square, square, whole((size, cut)), half, whole((size, cut))],
        out_specs=[half, square],
        compiler_params=params("arbitrary"),
        cost_estimate=prune_cost(size, cut, 6),
        name="prune",
    )(own, other, error, down, kept)


def prune_next(inverse, error, down, kept, cut, at):
    size = inverse.shape[0]
    half = pl.BlockSpec((size, cut), lambda i: (0, at))
    return pl.pallas_call(
        correct_kernel,
        out_shape=jax.ShapeDtypeStruct((size, cut), BF),
        grid=(1,),
        in_specs=[whole((size, size)), whole((size, cut)), half, whole((size, cut))],
        out_specs=whole((size, cut)),
        compiler_params=params("arbitrary"),
        cost_estimate=prune_cost(size, cut, 0),
        name="prune_next",
    )(inverse, error, down, kept)


def stage_kernel(*refs):
    count = len(refs) // 2
    for given, out in zip(refs[:count], refs[count:]):
        out[...] = given[...]


def stage(arrays):
    rows, width = arrays[0].shape
    spec = pl.BlockSpec((CHUNK, width), lambda i: (i, 0))
    return pl.pallas_call(
        stage_kernel,
        out_shape=[jax.ShapeDtypeStruct(a.shape, a.dtype) for a in arrays],
        grid=(rows // CHUNK,),
        in_specs=[spec] * len(arrays),
        out_specs=[spec] * len(arrays),
        compiler_params=params("arbitrary"),
        name="stage",
    )(*arrays)


def tied(values):
    return lax.optimization_barrier(values)


def outputs_kernel(block, arrived, own_hidden, other_hidden, own_ref, other_ref, *refs):
    total = dot(own_hidden[...], own_ref[...]) + dot(other_hidden[...], other_ref[...])
    first, second = total[:block], total[block:]
    if arrived:
        size = refs[0].shape[0]
        from_right, from_left = refs[0][...].astype(F32), refs[1][...].astype(F32)
        if size < block:
            empty = jnp.zeros((block - size, total.shape[1]), F32)
            from_left = jnp.concatenate([from_left, empty], axis=0)
            from_right = jnp.concatenate([empty, from_right], axis=0)
        first, second = first + from_right, second + from_left
    refs[-2][...] = first.astype(BF)
    refs[-1][...] = second.astype(BF)


def column_specs(hidden, rows, ff):
    return [pl.BlockSpec((rows, ff), lambda i, at=at: (0, at)) for _, at in hidden]


def outputs(hidden, own, other, arrived):
    rows = hidden[0][0].shape[0]
    ff, cut = own.shape
    given = (hidden[0][0], hidden[1][0], own, other) + arrived
    return pl.pallas_call(
        functools.partial(outputs_kernel, rows // 2, len(arrived)),
        out_shape=[jax.ShapeDtypeStruct((rows // 2, cut), BF)] * 2,
        grid=(1,),
        in_specs=column_specs(hidden, rows, ff) + [whole(g.shape) for g in given[2:]],
        out_specs=[whole((rows // 2, cut))] * 2,
        compiler_params=params("arbitrary"),
        cost_estimate=pl.CostEstimate(
            flops=4 * rows * own.shape[0] * cut,
            bytes_accessed=sum(g.size * 2 for g in given) + rows * cut * 2,
            transcendentals=0,
        ),
        name="outputs",
    )(*given)


def self_kernel(own_hidden, other_hidden, own_ref, other_ref, out_ref):
    out_ref[...] = dot(own_hidden[...], own_ref[...]) + dot(other_hidden[...], other_ref[...])


def self_outputs(hidden, own, other):
    rows, ff, cut = hidden[0][0].shape[0], *own.shape
    given = (hidden[0][0], hidden[1][0], own, other)
    return pl.pallas_call(
        self_kernel,
        out_shape=jax.ShapeDtypeStruct((rows, cut), F32),
        grid=(1,),
        in_specs=column_specs(hidden, rows, ff) + [whole(own.shape)] * 2,
        out_specs=whole((rows, cut)),
        compiler_params=params("arbitrary"),
        name="self_outputs",
    )(*given)


def finish_kernel(own_ref, right_ref, left_ref, *refs):
    total = own_ref[...] + right_ref[...].astype(F32) + left_ref[...].astype(F32)
    refs[-1][...] = total.astype(BF)


def finish(own, right, left, width, at, result):
    rows, cut = own.shape
    given = (own, right, left) + (() if result is None else (result,))
    return pl.pallas_call(
        finish_kernel,
        out_shape=jax.ShapeDtypeStruct((rows, width), BF),
        grid=(1,),
        in_specs=[whole((rows, cut))] * 3
        + ([] if result is None else [pl.BlockSpec(memory_space=pl.ANY)]),
        out_specs=pl.BlockSpec((rows, cut), lambda i: (0, at)),
        input_output_aliases={} if result is None else {3: 0},
        compiler_params=params("arbitrary"),
        name="finish",
    )(*given)


def ring_of(expert_size, mp_size):
    chips = mp_size // 2
    order = [(z, 0) for z in range(expert_size)]
    for z in reversed(range(expert_size)):
        side = list(range(1, chips)) if (expert_size - 1 - z) % 2 == 0 else list(range(chips - 1, 0, -1))
        order += [(z, x) for x in side]
    return [z * mp_size + 2 * x for z, x in order]


def dense(expert_size, mp_size, tokens, expert_ids, route_weights, gate, up, down, code):
    gate, up, down, code = gate[0], up[0], down[0], code[0]
    tok_rows, width = tokens.shape
    devices = expert_size * mp_size
    ring = ring_of(expert_size, mp_size)
    length = len(ring)
    reach = length // 2
    here = lax.axis_index(AXES)

    def shift(value, by):
        pairs = [
            (ring[i] + c, ring[(i + by) % length] + c) for i in range(length) for c in range(2)
        ]
        return lax.ppermute(value, AXES, pairs)

    def swap(value):
        return lax.ppermute(value, AXES, [(i, i ^ 1) for i in range(devices)])

    place = jnp.stack([here, here ^ 1]).astype(jnp.int32)
    top_wide, bottom_wide, bottom, top = split(tokens, expert_ids, route_weights, devices)

    def hop_first(hop):
        right[0], left[1] = shift(right[0], 1), shift(left[1], -1)
        if hop == reach:
            groups.append(((right[0], left[1]), (0,)))

    def hop_second(hop):
        right[1], left[0] = shift(right[1], 1), shift(left[0], -1)
        groups.append(((*right, *left), (0, 3)))

    top_wide, bottom_wide, gate_sent, up_sent = tied((top_wide, bottom_wide, gate, up))
    pairs = [(gate, up), (swap(gate_sent), swap(up_sent))]
    right, left = [top_wide, bottom], [top, bottom_wide]
    groups = [((top_wide, bottom), (0,))]
    grams = []
    hidden = []

    def work(hop):
        value, *after = hidden_part(place, (0, 1), devices, *groups[hop], pairs, grams)
        grams[:] = after
        hidden.append(((value, 0), (value, 1)))

    hop_first(1)
    cut = width // 2
    masked = [None, None]
    right[1], left[0], *pairs[1] = tied((right[1], left[0], *pairs[1]))
    hop_second(1)
    hop_first(2)
    pairs[1] = stage(pairs[1])
    right[1], left[0], *_ = tied((right[1], left[0], *pairs[1]))
    hop_second(2)
    for hop in range(3, reach + 1):
        while len(hidden) < (1 if hop == 3 else hop - 1):
            work(len(hidden))
        right[0], left[1], *grams = tied((right[0], left[1], *grams))
        hop_first(hop)
        if hop < reach:
            while len(hidden) < hop - 1:
                work(len(hidden))
            right[1], left[0], *grams = tied((right[1], left[0], *grams))
            hop_second(hop)
    masked = [masks(code, down, cut, at, 16) for at in range(2)]
    grams[0], *_ = tied((grams[0], *masked[0], *masked[1]))
    while len(hidden) < reach:
        work(len(hidden))
    grams = list(tied(tuple(grams)))
    last_other, gram_other = hidden_part(
        place, (1,), devices, *groups[reach], pairs[1:], grams[1:]
    )
    gram_other = swap(gram_other)
    last_own, gram_own = hidden_part(place, (0,), devices, *groups[reach], pairs[:1], grams[:1])
    hidden.append(((last_own, 0), (last_other, 0)))
    pruned = [None, None]
    (kept, error), (kept_next, error_next) = masked
    pruned[0], inverse = prune_first(gram_own, gram_other, error, down, kept, cut)
    pruned_other = [swap(pruned[0]), None]
    pruned[1] = prune_next(inverse, error_next, down, kept_next, cut, 1)
    pruned_other[1] = swap(pruned[1])

    moving = [(), ()]
    for hop in range(reach, 0, -1):
        for at in range(2):
            sent = outputs(hidden[hop], pruned[at], pruned_other[at], moving[at])
            go_left, go_right = sent if hop < reach else (sent[1], sent[0])
            moving[at] = (shift(go_left, -1), shift(go_right, 1))
    mixed = None
    for at in range(2):
        own = self_outputs(hidden[0], pruned[at], pruned_other[at])
        mixed = finish(own, *moving[at], width, at, mixed)
    return mixed, jnp.concatenate(pruned, axis=1)[None]


def local(expert_size, mp_size, section_size, *given):
    tokens, expert_ids, _, gate_weight = given[:4]
    devices = expert_size * mp_size
    if (
        section_size == 1
        and gate_weight.shape[0] == 1
        and 2 * expert_ids.shape[1] >= devices
        and mp_size % 2 == 0
        and devices >= 16
        and devices % EXTRA == 0
        and expert_ids.shape[0] == 128
        and 2 * devices * 128 <= EXTRA * tokens.shape[1]
    ):
        return dense(expert_size, mp_size, *given)
    return routed(*given)


def solution(mesh):
    placed = (
        P(("groups", "expert", "mp"), "section"),
        P(("groups", "expert", "mp"), None),
        P(("groups", "expert", "mp"), None),
        P(("expert", "mp"), "section", None),
        P(("expert", "mp"), "section", None),
        P(("expert", "mp"), None, "section"),
        P(("expert", "mp"), None, "section"),
    )
    sizes = mesh.shape
    return jax.shard_map(
        functools.partial(local, sizes["expert"], sizes["mp"], sizes["section"]),
        mesh=mesh,
        in_specs=placed,
        out_specs=(
            P(("groups", "expert", "mp"), "section"),
            P(("groups", "expert", "mp"), None, "section"),
        ),
        check_vma=False,
    )
```

```python
import functools
import jax
import jax.numpy as jnp
import numpy as np
from jax import lax
from jax.experimental import pallas as pl
from jax.experimental.pallas import tpu as pltpu
from jax.sharding import PartitionSpec as P

FF = 384
NS = 4


DAMPING = 0.01
EPSILON = 1e-06


def decode(mask_code):
    first_row = (mask_code <= 2).astype(jnp.float32)
    second_row = ((mask_code == 0) | (mask_code == 3) | (mask_code == 4)).astype(jnp.float32)
    third_row = ((mask_code == 1) | (mask_code == 3) | (mask_code == 5)).astype(jnp.float32)
    fourth_row = ((mask_code == 2) | (mask_code == 4) | (mask_code == 5)).astype(jnp.float32)
    kept_mask = jnp.stack([first_row, second_row, third_row, fourth_row], axis=2)
    return kept_mask.reshape(mask_code.shape[0], mask_code.shape[1] * 4, mask_code.shape[2])


def precise_matmul(left, right):
    return jnp.einsum(
        "jab,jbc->jac",
        left,
        right,
        precision=lax.Precision.HIGHEST,
        preferred_element_type=jnp.float32,
    )


def routed(tokens, expert_ids, route_weights, gate_weight, up_weight, down_weight, mask_code):
    group_count = lax.axis_size(("expert", "mp"))
    experts_here, half_rows, model_width = gate_weight.shape
    tok_rows, top_count = expert_ids.shape
    experts_all = experts_here * group_count
    capacity = min(tok_rows, 5 * tok_rows * top_count // (4 * experts_all))
    slot_total = group_count * capacity
    flat_ids = expert_ids.reshape(-1)
    onehot = (flat_ids[:, None] == jnp.arange(experts_all, dtype=jnp.int32)[None, :]).astype(
        jnp.int32
    )
    slot_rank = jnp.sum((jnp.cumsum(onehot, axis=0) - onehot) * onehot, axis=1)
    local_expert = flat_ids % experts_here
    position = flat_ids // experts_here * capacity + slot_rank
    token_of = jnp.arange(tok_rows * top_count, dtype=jnp.int32) // top_count
    slot_token = (
        jnp.full((experts_here, slot_total), tok_rows, jnp.int32)
        .at[local_expert, position]
        .set(token_of)
    )
    full_rows = lax.all_gather(tokens, "section", axis=1, tiled=True)
    padded_rows = jnp.concatenate(
        [full_rows, jnp.zeros((1, full_rows.shape[1]), full_rows.dtype)], axis=0
    )
    send_rows = padded_rows[slot_token]
    slot_rows = lax.all_to_all(send_rows, ("expert", "mp"), split_axis=1, concat_axis=1, tiled=True)
    gate_pre = jnp.einsum(
        "jfd,jsd->jfs", gate_weight, slot_rows, preferred_element_type=jnp.float32
    )
    up_pre = jnp.einsum("jfd,jsd->jfs", up_weight, slot_rows, preferred_element_type=jnp.float32)
    hidden_half = (jax.nn.silu(gate_pre) * up_pre).astype(jnp.bfloat16)
    hidden_all = lax.all_gather(hidden_half, "section", axis=1, tiled=True)
    hidden_width = hidden_all.shape[1]
    gram_matrix = jnp.einsum(
        "jfs,jgs->jfg", hidden_all, hidden_all, preferred_element_type=jnp.float32
    )
    mean_diag = jnp.mean(jnp.diagonal(gram_matrix, axis1=1, axis2=2), axis=1)
    identity = jnp.eye(hidden_width, dtype=jnp.float32)
    hessian = gram_matrix + (DAMPING * mean_diag + EPSILON)[:, None, None] * identity
    step_size = 1.0 / jnp.max(jnp.sum(jnp.abs(hessian), axis=2), axis=1)
    iterate = (
        2.0 * step_size[:, None, None] * identity - (step_size * step_size)[:, None, None] * hessian
    )
    for iteration in range(NS - 1):
        iterate = 2.0 * iterate - precise_matmul(precise_matmul(iterate, hessian), iterate)
    kept_mask = decode(mask_code)
    weight_wide = down_weight.astype(jnp.float32)
    inverse_diag = jnp.diagonal(iterate, axis1=1, axis2=2)
    scaled_error = weight_wide * (1.0 - kept_mask) / inverse_diag[:, :, None]
    correction = precise_matmul(iterate, scaled_error)
    pruned = (kept_mask * (weight_wide - correction)).astype(jnp.bfloat16)
    expert_out = (
        jnp.einsum("jfs,jfd->jsd", hidden_all, pruned, preferred_element_type=jnp.float32)
        * FF ** (-0.5)
    ).astype(jnp.bfloat16)
    returned = lax.all_to_all(expert_out, ("expert", "mp"), split_axis=1, concat_axis=1, tiled=True)
    picked = returned[local_expert, position].reshape(tok_rows, top_count, -1)
    combined = jnp.einsum("tkd,tk->td", picked.astype(jnp.float32), route_weights)
    return (combined.astype(jnp.bfloat16), pruned)


AXES = ("expert", "mp")
CHUNK = 128
EXTRA = 8
BF = jnp.bfloat16
F32 = jnp.float32


def params(*semantics, mib=16):
    return pltpu.CompilerParams(
        dimension_semantics=semantics or None, vmem_limit_bytes=mib * 1024 * 1024
    )


def whole(shape):
    return pl.BlockSpec(shape, lambda *_: (0,) * len(shape))


def dot(left, right, on=((1,), (0,))):
    return lax.dot_general(left, right, (on, ((), ())), preferred_element_type=F32)


def split_kernel(experts_all, x_ref, ids_ref, weight_ref, *out_refs):
    half = x_ref.shape[0] // 2
    ids, weight = ids_ref[...], weight_ref[...]
    table = [
        jnp.max(jnp.where(ids == e, weight, -1.0), axis=0, keepdims=True)
        for e in range(experts_all)
    ]
    table = jnp.concatenate(table, axis=0)
    high = table.astype(BF).astype(F32)
    both = jnp.concatenate([high, table - high], axis=0)
    parts = [both[i : i + EXTRA] for i in range(0, 2 * experts_all, EXTRA)]
    lanes = both.shape[1]
    rest = x_ref.shape[1] - len(parts) * lanes
    extra = jnp.concatenate(parts + [jnp.zeros((EXTRA, rest), F32)], axis=1).astype(BF)
    for at, (wide, plain) in enumerate(((out_refs[0], out_refs[3]), (out_refs[1], out_refs[2]))):
        value = x_ref[at * half : (at + 1) * half, :]
        wide[:half, :] = value
        wide[half:, :] = extra
        plain[...] = value


def split(tokens, expert_ids, route_weights, experts_all):
    rows, width = tokens.shape
    wide = jax.ShapeDtypeStruct((rows // 2 + EXTRA, width), BF)
    plain = jax.ShapeDtypeStruct((rows // 2, width), BF)
    given = (tokens, expert_ids.T, route_weights.T)
    return pl.pallas_call(
        functools.partial(split_kernel, experts_all),
        out_shape=[wide, wide, plain, plain],
        grid=(1,),
        in_specs=[whole(g.shape) for g in given],
        out_specs=[whole(o.shape) for o in (wide, wide, plain, plain)],
        compiler_params=params("arbitrary", mib=56),
        name="split",
    )(*given)


def token_weights(ref, experts_all, expert):
    half, lanes = ref.shape[0] - EXTRA, 2 * (ref.shape[0] - EXTRA)
    count = 2 * experts_all // EXTRA
    parts = [ref[half:, i * lanes : (i + 1) * lanes].astype(F32) for i in range(count)]
    both = jnp.concatenate(parts, axis=0)
    table = both[:experts_all] + both[experts_all:]
    row = lax.broadcasted_iota(jnp.int32, table.shape, 0)
    return jnp.sum(jnp.where(row == expert, table, 0.0), axis=0, keepdims=True)


def mask_kernel(code_ref, down_ref, kept_ref, error_ref):
    rows, groups = down_ref.shape[0], code_ref.shape[0]
    code = code_ref[...]
    first = code <= 2
    second = (code == 0) | (code == 3) | (code == 4)
    third = (code == 1) | (code == 3) | (code == 5)
    fourth = (code == 2) | (code == 4) | (code == 5)
    planes = [jnp.where(plane, 1.0, 0.0).astype(BF) for plane in (first, second, third, fourth)]
    row = lax.broadcasted_iota(jnp.int32, (rows, rows), 0)
    column = lax.broadcasted_iota(jnp.int32, (rows, rows), 1)
    spread = jnp.where(row % 4 * groups + row // 4 == column, 1.0, 0.0).astype(BF)
    kept = dot(spread, jnp.concatenate(planes, axis=0))
    kept_ref[...] = kept.astype(BF)
    error_ref[...] = jnp.where(kept > 0.5, 0.0, down_ref[...].astype(F32)).astype(BF)


def masks(code, down, cut, at, mib):
    groups, width = code.shape
    rows = down.shape[0]
    step = cut // 2
    first = at * 2
    taken = pl.BlockSpec((rows, step), lambda i: (0, i + first))
    given = pl.BlockSpec((rows, step), lambda i: (0, i))
    return pl.pallas_call(
        mask_kernel,
        out_shape=[jax.ShapeDtypeStruct((rows, cut), BF)] * 2,
        grid=(2,),
        in_specs=[pl.BlockSpec((groups, step), lambda i: (0, i + first)), taken],
        out_specs=[given, given],
        compiler_params=params("arbitrary", mib=mib),
        cost_estimate=pl.CostEstimate(
            flops=2 * rows * rows * cut, bytes_accessed=8 * rows * cut, transcendentals=0
        ),
        name="masks",
    )(code, down)


def hidden_kernel(pieces, sources, experts, experts_all, has_gram, place_ref, *refs):
    count = len(experts)
    x_refs, refs = refs[:pieces], refs[pieces:]
    pairs, grams_in = refs[: 2 * count], refs[2 * count : 3 * count]
    out_ref, gram_refs, rows_ref = refs[-2 - count], refs[-1 - count : -1], refs[-1]
    half = min(x.shape[0] for x in x_refs)
    half = half - half % 16
    for at, x in enumerate(x_refs):
        rows_ref[at * half : (at + 1) * half, :] = x[:half, :]
    for which in range(count):
        gate_ref, up_ref = pairs[2 * which], pairs[2 * which + 1]
        ff = gate_ref.shape[0]
        weight = [
            token_weights(x_refs[i], experts_all, place_ref[experts[which]]) for i in sources
        ]
        empty = jnp.zeros((8 - len(sources), weight[0].shape[1]), F32)
        weight = jnp.concatenate(weight + [empty], axis=0).T
        weight = jnp.concatenate([weight[:, at : at + 1] for at in range(len(sources))], axis=0)
        parts = []
        for at in range(0, ff, CHUNK):
            both = [gate_ref[at : at + CHUNK, :], up_ref[at : at + CHUNK, :]]
            pre = dot(rows_ref[...], jnp.concatenate(both, axis=0), ((1,), (1,)))
            gate, up = pre[:, :CHUNK], pre[:, CHUNK:]
            value = gate / (1.0 + jnp.exp(-gate)) * up
            value = jnp.where(weight >= 0.0, value, 0.0).astype(BF)
            column = which * ff + at
            out_ref[:, column : column + CHUNK] = (
                value.astype(F32) * (weight * FF ** (-0.5))
            ).astype(BF)
            parts.append(value)
        hidden = jnp.concatenate(parts, axis=1)
        gram = dot(hidden, hidden, ((0,), (0,)))
        gram_refs[which][...] = grams_in[which][...] + gram if has_gram else gram


def hidden_part(place, experts, experts_all, pieces, sources, pairs, grams):
    half = min(p.shape[0] for p in pieces)
    rows = len(pieces) * (half - half % 16)
    ff, width = pairs[0][0].shape
    count = len(experts)
    resident = pl.BlockSpec(memory_space=pltpu.VMEM)
    given = [*pieces] + [w for pair in pairs for w in pair] + [*grams]
    return pl.pallas_call(
        functools.partial(
            hidden_kernel, len(pieces), sources, experts, experts_all, len(grams) > 0
        ),
        out_shape=[jax.ShapeDtypeStruct((rows, count * ff), BF)]
        + [jax.ShapeDtypeStruct((ff, ff), F32)] * count,
        in_specs=[pl.BlockSpec(memory_space=pltpu.SMEM)] + [resident] * len(given),
        out_specs=[resident] * (1 + count),
        scratch_shapes=[pltpu.VMEM((rows, width), BF)],
        compiler_params=params(),
        cost_estimate=pl.CostEstimate(
            flops=4 * rows * ff * width * count,
            bytes_accessed=2 * (rows + 2 * ff * count) * width,
            transcendentals=rows * ff * count,
        ),
        name="hidden",
    )(place, *given)


def product(left, right):
    return dot(left.astype(BF), right)


def prune_kernel(own_ref, other_ref, error_ref, down_ref, kept_ref, out_ref, inverse_ref):
    gram = own_ref[...] + other_ref[...]
    size = gram.shape[0]
    row = lax.broadcasted_iota(jnp.int32, (size, size), 0)
    column = lax.broadcasted_iota(jnp.int32, (size, size), 1)
    eye = row == column
    mean_diag = jnp.sum(jnp.where(eye, gram, 0.0)) * (1.0 / size)
    hessian = gram + jnp.where(eye, DAMPING * mean_diag + EPSILON, 0.0)
    step_size = 1.0 / jnp.max(jnp.sum(jnp.abs(hessian), axis=0, keepdims=True))
    scaled = step_size * hessian
    iterate = jnp.where(eye, 2.0, 0.0) - scaled
    right = scaled.astype(BF)
    scaled = 2.0 * scaled - dot(right, right)
    for iteration in range(NS - 1):
        right = scaled.astype(BF)
        following = 2.0 * iterate - product(iterate, right)
        if iteration < NS - 2:
            scaled = 2.0 * scaled - dot(right, right)
        iterate = following
    diag = jnp.sum(jnp.where(eye, iterate, 0.0), axis=0, keepdims=True)
    inverse_ref[...] = (iterate * (1.0 / diag)).astype(BF)
    correct_kernel(inverse_ref, error_ref, down_ref, kept_ref, out_ref)


def correct_kernel(inverse_ref, error_ref, down_ref, kept_ref, out_ref):
    correction = dot(inverse_ref[...], error_ref[...])
    value = kept_ref[...].astype(F32) * (down_ref[...].astype(F32) - correction)
    out_ref[...] = value.astype(BF)


def prune_cost(size, cut, products):
    return pl.CostEstimate(
        flops=2 * size * size * (cut + products * size),
        bytes_accessed=8 * size * cut + 8 * size * size,
        transcendentals=0,
    )


def prune_first(own, other, error, down, kept, cut):
    size = own.shape[0]
    half = pl.BlockSpec((size, cut), lambda i: (0, 0))
    square = whole((size, size))
    return pl.pallas_call(
        prune_kernel,
        out_shape=[
            jax.ShapeDtypeStruct((size, cut), BF),
            jax.ShapeDtypeStruct((size, size), BF),
        ],
        grid=(1,),
        in_specs=[square, square, whole((size, cut)), half, whole((size, cut))],
        out_specs=[half, square],
        compiler_params=params("arbitrary"),
        cost_estimate=prune_cost(size, cut, 6),
        name="prune",
    )(own, other, error, down, kept)


def prune_next(inverse, error, down, kept, cut, at):
    size = inverse.shape[0]
    half = pl.BlockSpec((size, cut), lambda i: (0, at))
    return pl.pallas_call(
        correct_kernel,
        out_shape=jax.ShapeDtypeStruct((size, cut), BF),
        grid=(1,),
        in_specs=[whole((size, size)), whole((size, cut)), half, whole((size, cut))],
        out_specs=whole((size, cut)),
        compiler_params=params("arbitrary"),
        cost_estimate=prune_cost(size, cut, 0),
        name="prune_next",
    )(inverse, error, down, kept)


def stage_kernel(*refs):
    count = len(refs) // 2
    for given, out in zip(refs[:count], refs[count:]):
        out[...] = given[...]


def stage(arrays):
    rows, width = arrays[0].shape
    spec = pl.BlockSpec((CHUNK, width), lambda i: (i, 0))
    return pl.pallas_call(
        stage_kernel,
        out_shape=[jax.ShapeDtypeStruct(a.shape, a.dtype) for a in arrays],
        grid=(rows // CHUNK,),
        in_specs=[spec] * len(arrays),
        out_specs=[spec] * len(arrays),
        compiler_params=params("arbitrary"),
        name="stage",
    )(*arrays)


def tied(values):
    return lax.optimization_barrier(values)


def outputs_kernel(block, arrived, own_hidden, other_hidden, own_ref, other_ref, *refs):
    total = dot(own_hidden[...], own_ref[...]) + dot(other_hidden[...], other_ref[...])
    first, second = total[:block], total[block:]
    if arrived:
        size = refs[0].shape[0]
        from_right, from_left = refs[0][...].astype(F32), refs[1][...].astype(F32)
        if size < block:
            empty = jnp.zeros((block - size, total.shape[1]), F32)
            from_left = jnp.concatenate([from_left, empty], axis=0)
            from_right = jnp.concatenate([empty, from_right], axis=0)
        first, second = first + from_right, second + from_left
    refs[-2][...] = first.astype(BF)
    refs[-1][...] = second.astype(BF)


def column_specs(hidden, rows, ff):
    return [pl.BlockSpec((rows, ff), lambda i, at=at: (0, at)) for _, at in hidden]


def outputs(hidden, own, other, arrived):
    rows = hidden[0][0].shape[0]
    ff, cut = own.shape
    given = (hidden[0][0], hidden[1][0], own, other) + arrived
    return pl.pallas_call(
        functools.partial(outputs_kernel, rows // 2, len(arrived)),
        out_shape=[jax.ShapeDtypeStruct((rows // 2, cut), BF)] * 2,
        grid=(1,),
        in_specs=column_specs(hidden, rows, ff) + [whole(g.shape) for g in given[2:]],
        out_specs=[whole((rows // 2, cut))] * 2,
        compiler_params=params("arbitrary"),
        cost_estimate=pl.CostEstimate(
            flops=4 * rows * own.shape[0] * cut,
            bytes_accessed=sum(g.size * 2 for g in given) + rows * cut * 2,
            transcendentals=0,
        ),
        name="outputs",
    )(*given)


def self_kernel(own_hidden, other_hidden, own_ref, other_ref, out_ref):
    out_ref[...] = dot(own_hidden[...], own_ref[...]) + dot(other_hidden[...], other_ref[...])


def self_outputs(hidden, own, other):
    rows, ff, cut = hidden[0][0].shape[0], *own.shape
    given = (hidden[0][0], hidden[1][0], own, other)
    return pl.pallas_call(
        self_kernel,
        out_shape=jax.ShapeDtypeStruct((rows, cut), F32),
        grid=(1,),
        in_specs=column_specs(hidden, rows, ff) + [whole(own.shape)] * 2,
        out_specs=whole((rows, cut)),
        compiler_params=params("arbitrary"),
        name="self_outputs",
    )(*given)


def finish_kernel(own_ref, right_ref, left_ref, *refs):
    total = own_ref[...] + right_ref[...].astype(F32) + left_ref[...].astype(F32)
    refs[-1][...] = total.astype(BF)


def finish(own, right, left, width, at, result):
    rows, cut = own.shape
    given = (own, right, left) + (() if result is None else (result,))
    return pl.pallas_call(
        finish_kernel,
        out_shape=jax.ShapeDtypeStruct((rows, width), BF),
        grid=(1,),
        in_specs=[whole((rows, cut))] * 3
        + ([] if result is None else [pl.BlockSpec(memory_space=pl.ANY)]),
        out_specs=pl.BlockSpec((rows, cut), lambda i: (0, at)),
        input_output_aliases={} if result is None else {3: 0},
        compiler_params=params("arbitrary"),
        name="finish",
    )(*given)


def ring_of(expert_size, mp_size):
    chips = mp_size // 2
    order = [(z, 0) for z in range(expert_size)]
    for z in reversed(range(expert_size)):
        side = list(range(1, chips)) if (expert_size - 1 - z) % 2 == 0 else list(range(chips - 1, 0, -1))
        order += [(z, x) for x in side]
    return [z * mp_size + 2 * x for z, x in order]


def dense(expert_size, mp_size, tokens, expert_ids, route_weights, gate, up, down, code):
    gate, up, down, code = gate[0], up[0], down[0], code[0]
    tok_rows, width = tokens.shape
    devices = expert_size * mp_size
    ring = ring_of(expert_size, mp_size)
    length = len(ring)
    reach = length // 2
    here = lax.axis_index(AXES)

    def shift(value, by):
        pairs = [
            (ring[i] + c, ring[(i + by) % length] + c) for i in range(length) for c in range(2)
        ]
        return lax.ppermute(value, AXES, pairs)

    def swap(value):
        return lax.ppermute(value, AXES, [(i, i ^ 1) for i in range(devices)])

    place = jnp.stack([here, here ^ 1]).astype(jnp.int32)
    top_wide, bottom_wide, bottom, top = split(tokens, expert_ids, route_weights, devices)

    def hop_first(hop):
        right[0], left[1] = shift(right[0], 1), shift(left[1], -1)
        if hop == reach:
            groups.append(((right[0], left[1]), (0,)))

    def hop_second(hop):
        right[1], left[0] = shift(right[1], 1), shift(left[0], -1)
        groups.append(((*right, *left), (0, 3)))

    top_wide, bottom_wide, gate_sent, up_sent = tied((top_wide, bottom_wide, gate, up))
    pairs = [(gate, up), (swap(gate_sent), swap(up_sent))]
    right, left = [top_wide, bottom], [top, bottom_wide]
    groups = [((top_wide, bottom), (0,))]
    grams = []
    hidden = []

    def work(hop):
        value, *after = hidden_part(place, (0, 1), devices, *groups[hop], pairs, grams)
        grams[:] = after
        hidden.append(((value, 0), (value, 1)))

    hop_first(1)
    cut = width // 2
    masked = [None, None]
    right[1], left[0], *pairs[1] = tied((right[1], left[0], *pairs[1]))
    hop_second(1)
    hop_first(2)
    pairs[1] = stage(pairs[1])
    own, gram_own = hidden_part(place, (0,), devices, *groups[0], pairs[:1], [])
    right[1], left[0], gram_own, *_ = tied((right[1], left[0], gram_own, *pairs[1]))
    hop_second(2)
    other, gram_other = hidden_part(place, (1,), devices, *groups[0], pairs[1:], [])
    hidden.append(((own, 0), (other, 0)))
    grams = [gram_own, gram_other]
    for hop in range(3, reach + 1):
        while len(hidden) < (1 if hop == 3 else hop - 1):
            work(len(hidden))
        right[0], left[1], *grams = tied((right[0], left[1], *grams))
        hop_first(hop)
        if hop < reach:
            while len(hidden) < hop - 1:
                work(len(hidden))
            right[1], left[0], *grams = tied((right[1], left[0], *grams))
            hop_second(hop)
    masked = [masks(code, down, cut, at, 16) for at in range(2)]
    grams[0], *_ = tied((grams[0], *masked[0], *masked[1]))
    while len(hidden) < reach:
        work(len(hidden))
    grams = list(tied(tuple(grams)))
    last_other, gram_other = hidden_part(
        place, (1,), devices, *groups[reach], pairs[1:], grams[1:]
    )
    gram_other = swap(gram_other)
    last_own, gram_own = hidden_part(place, (0,), devices, *groups[reach], pairs[:1], grams[:1])
    hidden.append(((last_own, 0), (last_other, 0)))
    pruned = [None, None]
    (kept, error), (kept_next, error_next) = masked
    pruned[0], inverse = prune_first(gram_own, gram_other, error, down, kept, cut)
    pruned_other = [swap(pruned[0]), None]
    pruned[1] = prune_next(inverse, error_next, down, kept_next, cut, 1)
    pruned_other[1] = swap(pruned[1])

    moving = [(), ()]
    for hop in range(reach, 0, -1):
        for at in range(2):
            sent = outputs(hidden[hop], pruned[at], pruned_other[at], moving[at])
            go_left, go_right = sent if hop < reach else (sent[1], sent[0])
            moving[at] = (shift(go_left, -1), shift(go_right, 1))
    mixed = None
    for at in range(2):
        own = self_outputs(hidden[0], pruned[at], pruned_other[at])
        mixed = finish(own, *moving[at], width, at, mixed)
    return mixed, jnp.concatenate(pruned, axis=1)[None]


def local(expert_size, mp_size, section_size, *given):
    tokens, expert_ids, _, gate_weight = given[:4]
    devices = expert_size * mp_size
    if (
        section_size == 1
        and gate_weight.shape[0] == 1
        and 2 * expert_ids.shape[1] >= devices
        and mp_size % 2 == 0
        and devices >= 16
        and devices % EXTRA == 0
        and expert_ids.shape[0] == 128
        and 2 * devices * 128 <= EXTRA * tokens.shape[1]
    ):
        return dense(expert_size, mp_size, *given)
    return routed(*given)


def solution(mesh):
    placed = (
        P(("groups", "expert", "mp"), "section"),
        P(("groups", "expert", "mp"), None),
        P(("groups", "expert", "mp"), None),
        P(("expert", "mp"), "section", None),
        P(("expert", "mp"), "section", None),
        P(("expert", "mp"), None, "section"),
        P(("expert", "mp"), None, "section"),
    )
    sizes = mesh.shape
    return jax.shard_map(
        functools.partial(local, sizes["expert"], sizes["mp"], sizes["section"]),
        mesh=mesh,
        in_specs=placed,
        out_specs=(
            P(("groups", "expert", "mp"), "section"),
            P(("groups", "expert", "mp"), None, "section"),
        ),
        check_vma=False,
    )
```
